512 devices in a mesh: seq: 32 (over x, z_hi, core), tile: 16 (over y, z_lo).
Axes of the slice: x: 4, y: 4, z: 16 (z_hi: 4, z_lo: 4; z = z_hi * 4 + z_lo), core: 2. Of those that a mesh axis runs over, the one named last changes fastest.
Arguments:
- queries: bfloat16 [65536, 2048], P(('seq', 'tile')), may hold values from -192 to 192
- head_keys: bfloat16 [65536, 2048], P(('seq', 'tile')), may hold values from -6 to 6
- head_values: bfloat16 [65536, 2048], P(('seq', 'tile')), may hold values from -12 to 12
- region_request: int32 [65536], P(('seq', 'tile')), may hold values from 0 to 7
- request_adapter: int32 [8], replicated, may hold values from 0 to 3
- residual: bfloat16 [65536, 3072], P(('seq', 'tile')), may hold values from -3 to 3
- output_gate: float32 [3072], replicated, may hold values from 0.1 to 1.9
- output_weight: bfloat16 [2048, 3072], P(None, 'tile'), may hold values from -1.5 to 1.5
- adapter_down_factors: bfloat16 [2048, 128], replicated, may hold values from -0.125 to 0.125
- adapter_up_factors: bfloat16 [128, 3072], P(None, 'tile'), may hold values from -1.5 to 1.5
- closing_scale: float32 [3072], replicated, may hold values from -2.5 to 2.5
- closing_shift: float32 [3072], replicated, may hold values from -2.5 to 2.5
- patch_projection_weight: bfloat16 [3072, 64], replicated, may hold values from -0.0546875 to 0.0546875
- patch_projection_bias: float32 [64], replicated, may hold values from -2.5 to 2.5
- convolution_kernel: bfloat16 [3, 3, 16, 512], replicated, may hold values from -0.5 to 0.5
- convolution_bias: float32 [512], replicated, may hold values from -2.5 to 2.5
Outputs:
- decoded: bfloat16 [512, 512, 512], P('seq', 'tile')
The draws below stay inside these ranges and needn't reach their ends.
All inputs are finite; a program needn't handle non-finite values.
Results may differ from the reference program's by a relative error of at most 0.015.
Values may be sent and summed in bfloat16 or wider, within the bound.
A program may use at most 64 MiB of HBM per device.

```python
import math
import jax
import jax.numpy as jnp
from jax import lax

MODEL_WIDTH = 3072
HD = 128
LAT_CH = 16
CONV = 512
ADAPTER_RANK = 32
ADAPTER_COUNT = 4
REQUESTS = 8
LAT_W = 256
WIN = 512
TOKENS = 65536
HEAD_FEATURES = 2048
PCH = 64


def draw_queries(key, part):
    key = jax.random.fold_in(key, 1)
    values = jnp.clip(jax.random.normal(key, (TOKENS, HEAD_FEATURES), jnp.float32), -6.0, 6.0)
    return values.astype(jnp.bfloat16)


def draw_head_keys(key, part):
    key = jax.random.fold_in(key, 2)
    values = jnp.clip(jax.random.normal(key, (TOKENS, HEAD_FEATURES), jnp.float32), -6.0, 6.0)
    return values.astype(jnp.bfloat16)


def draw_residual(key, part):
    key = jax.random.fold_in(key, 3)
    values = jnp.clip(0.5 * jax.random.normal(key, (TOKENS, MODEL_WIDTH), jnp.float32), -3.0, 3.0)
    return values.astype(jnp.bfloat16)


def draw_output_weight(key, part):
    key = jax.random.fold_in(key, 4)
    spread_factor = 1.0 / math.sqrt(float(HEAD_FEATURES // 16))
    values = jnp.clip(jax.random.normal(key, (HEAD_FEATURES, MODEL_WIDTH), jnp.float32), -6.0, 6.0) * spread_factor
    values = jnp.clip(values, -1.5, 1.5)
    return values.astype(jnp.bfloat16)


def draw_adapter_up_factors(key, part):
    key = jax.random.fold_in(key, 5)
    values = jnp.clip(0.25 * jax.random.normal(key, (ADAPTER_COUNT * ADAPTER_RANK, MODEL_WIDTH), jnp.float32), -1.5, 1.5)
    return values.astype(jnp.bfloat16)


def place_ends(entries, own_key, least, high):
    longest = entries.shape.index(max(entries.shape))
    spots = []
    for shift in (0, 1):
        where = [jax.random.randint(jax.random.fold_in(own_key, axis), (), 0, length) for axis, length in enumerate(entries.shape)]
        where[longest] = (where[longest] + shift) % entries.shape[longest]
        spots.append(tuple(where))
    return entries.at[spots[0]].set(least).at[spots[1]].set(high)


def shard_levels(rng, extent, cuts, least, largest):
    loudness, own = 1.0, jax.random.fold_in(rng, 6)
    for axis_at, blocks in cuts:
        draws = jnp.exp(jax.random.uniform(jax.random.fold_in(own, axis_at), (blocks,), jnp.float32, least / len(cuts), largest / len(cuts)))
        loudness = loudness * jnp.repeat(draws, extent[axis_at] // blocks).reshape([-1 if axis == axis_at else 1 for axis in range(len(extent))])
    return loudness


def normal_values(own_key, shape, deviation, bound, cuts=(), held_as=jnp.bfloat16):
    drawn = jax.random.normal(own_key, shape, jnp.float32) * deviation
    if len(cuts) > 0:
        drawn = shard_levels(own_key, shape, cuts, -0.22, 0.18) * drawn
    return jnp.clip(drawn, min=-bound, max=bound).astype(held_as)


def setup_inputs(seed: int = 0) -> dict:
    key_of = jax.random.split(jax.random.key(seed), 17)
    return {
        "queries": draw_queries(jax.random.fold_in(key_of[16], 71), 0),
        "head_keys": draw_head_keys(jax.random.fold_in(key_of[16], 71), 0),
        "head_values": normal_values(key_of[2], (TOKENS, HEAD_FEATURES), 2.0, 12.0, ((0, 512),)),
        "region_request": place_ends(jax.random.randint(key_of[3], (TOKENS,), 0, REQUESTS), jax.random.fold_in(key_of[3], 1), 0, REQUESTS - 1).astype(jnp.int32),
        "request_adapter": place_ends(jax.random.randint(key_of[4], (REQUESTS,), 0, ADAPTER_COUNT), jax.random.fold_in(key_of[4], 1), 0, ADAPTER_COUNT - 1).astype(jnp.int32),
        "residual": draw_residual(jax.random.fold_in(key_of[16], 71), 0),
        "output_gate": jnp.clip(1.0 + 0.18 * jax.random.normal(key_of[6], (MODEL_WIDTH,), jnp.float32), 0.1, 1.9),
        "output_weight": draw_output_weight(jax.random.fold_in(key_of[16], 71), 0),
        "adapter_down_factors": normal_values(key_of[8], (HEAD_FEATURES, ADAPTER_COUNT * ADAPTER_RANK), HEAD_FEATURES ** -0.5, 0.125),
        "adapter_up_factors": draw_adapter_up_factors(jax.random.fold_in(key_of[16], 71), 0),
        "closing_scale": normal_values(key_of[10], (MODEL_WIDTH,), 0.5, 2.5, (), jnp.float32),
        "closing_shift": normal_values(key_of[11], (MODEL_WIDTH,), 0.5, 2.5, (), jnp.float32),
        "patch_projection_weight": normal_values(key_of[12], (MODEL_WIDTH, PCH), (4 * MODEL_WIDTH) ** -0.5, 0.0546875),
        "patch_projection_bias": normal_values(key_of[13], (PCH,), 0.5, 2.5, (), jnp.float32),
        "convolution_kernel": normal_values(key_of[14], (3, 3, LAT_CH, CONV), (9 * LAT_CH) ** -0.5, 0.5),
        "convolution_bias": normal_values(key_of[15], (CONV,), 0.5, 2.5, (), jnp.float32),
    }


norm_epsilon = 1e-06
latent_scaling = 0.3611
latent_offset = 0.1159

def band_attention(queries, key_rows, value_rows, first_token, token_total, window, head_size):
    row_count = queries.shape[0]
    block_rows = min(512, row_count)
    scaling = 1.0 / math.sqrt(head_size)

    def one_block(block_index):
        first_row = block_index * block_rows
        query_block = lax.dynamic_slice_in_dim(queries, first_row, block_rows, 0).astype(jnp.float32)
        key_block = lax.dynamic_slice_in_dim(key_rows, first_row, block_rows + 2 * window, 0).astype(jnp.float32)
        value_block = lax.dynamic_slice_in_dim(value_rows, first_row, block_rows + 2 * window, 0).astype(jnp.float32)
        scores = jnp.einsum('qhd,khd->hqk', query_block, key_block) * scaling
        query_place = first_token + first_row + jnp.arange(block_rows, dtype=jnp.int32)
        key_place = first_token - window + first_row + jnp.arange(block_rows + 2 * window, dtype=jnp.int32)
        distance = jnp.abs(query_place[:, None] - key_place[None, :])
        allowed = (distance <= window) & (key_place[None, :] >= 0) & (key_place[None, :] < token_total)
        scores = jnp.where(allowed[None], scores, -jnp.inf)
        highest = lax.optimization_barrier(jnp.max(scores, axis=2, keepdims=True))
        expons = jnp.exp(scores - highest)
        totals = lax.optimization_barrier(jnp.sum(expons, axis=2))
        weights = lax.optimization_barrier(expons.astype(jnp.bfloat16)).astype(jnp.float32)
        weighted = jnp.einsum('hqk,khd->qhd', weights, value_block)
        return (weighted / jnp.transpose(totals)[:, :, None]).astype(jnp.bfloat16)
    pieces = lax.map(one_block, jnp.arange(row_count // block_rows, dtype=jnp.int32))
    return pieces.reshape(row_count, -1)

def adapter_of(region_request, request_adapter):
    request_cols = jnp.arange(request_adapter.shape[0], dtype=jnp.int32)
    matches = region_request[:, None] == request_cols[None, :]
    return lax.optimization_barrier(jnp.sum(jnp.where(matches, request_adapter[None, :], 0), axis=1)).astype(jnp.int32)

def reduced_rank(attended_heads, adapter_down_factors, adapter_list, rank_width):
    lowered_result = jnp.dot(attended_heads, adapter_down_factors, preferred_element_type=jnp.float32)
    owner_requests = jnp.arange(adapter_down_factors.shape[1], dtype=jnp.int32) // rank_width
    kept_cols = adapter_list[:, None] == owner_requests[None, :]
    return jnp.where(kept_cols, lowered_result, 0.0).astype(jnp.bfloat16)

def patch_latents(block_out, closing_scale, closing_shift, patch_projection_weight, patch_projection_bias):
    block_values = block_out.astype(jnp.float32)
    average = lax.optimization_barrier(jnp.mean(block_values, axis=1, keepdims=True))
    centered = block_values - average
    variance = lax.optimization_barrier(jnp.mean(centered * centered, axis=1, keepdims=True))
    modulated = (centered * lax.rsqrt(variance + norm_epsilon) * (1.0 + closing_scale) + closing_shift).astype(jnp.bfloat16)
    projected = jnp.dot(modulated, patch_projection_weight, preferred_element_type=jnp.float32) + patch_projection_bias
    return (projected / latent_scaling + latent_offset).astype(jnp.bfloat16)

def unpatch(latent_rows, token_rows, token_cols, channels):
    shaped = latent_rows.reshape(token_rows, token_cols, channels, 2, 2)
    return jnp.transpose(shaped, (0, 3, 1, 4, 2)).reshape(2 * token_rows, 2 * token_cols, channels)

def conv_apply(padded, convolution_kernel, convolution_bias):
    height = padded.shape[0] - 2
    breadth = padded.shape[1] - 2
    shifted = [padded[row_step:row_step + height, col_step:col_step + breadth] for row_step in range(3) for col_step in range(3)]
    stacked = jnp.concatenate(shifted, axis=2).reshape(height * breadth, -1)
    flat_weight = convolution_kernel.reshape(-1, convolution_kernel.shape[3])
    output = jnp.dot(stacked, flat_weight, preferred_element_type=jnp.float32) + convolution_bias
    return output.reshape(height, breadth, -1).astype(jnp.bfloat16)

def reference(queries, head_keys, head_values, region_request, request_adapter, residual, output_gate, output_weight, adapter_down_factors, adapter_up_factors, closing_scale, closing_shift, patch_projection_weight, patch_projection_bias, convolution_kernel, convolution_bias):
    head_count = HEAD_FEATURES // HD
    padding = ((WIN, WIN), (0, 0), (0, 0))
    query_heads = queries.reshape(TOKENS, head_count, HD)
    key_heads = jnp.pad(head_keys.reshape(TOKENS, head_count, HD), padding)
    value_heads = jnp.pad(head_values.reshape(TOKENS, head_count, HD), padding)
    attended_heads = band_attention(query_heads, key_heads, value_heads, 0, TOKENS, WIN, HD)
    adapter_list = adapter_of(region_request, request_adapter)
    group_rows = math.gcd(TOKENS, 4096)

    def finish_rows(position):
        first_row = position * group_rows
        attention_rows = lax.dynamic_slice_in_dim(attended_heads, first_row, group_rows, 0)
        residual_rows = lax.dynamic_slice_in_dim(residual, first_row, group_rows, 0)
        adapter_matrix_rows = lax.dynamic_slice_in_dim(adapter_list, first_row, group_rows, 0)
        lowered_result = reduced_rank(attention_rows, adapter_down_factors, adapter_matrix_rows, ADAPTER_RANK)
        branch_output = jnp.dot(attention_rows, output_weight, preferred_element_type=jnp.float32) + jnp.dot(lowered_result, adapter_up_factors, preferred_element_type=jnp.float32)
        block_out = lax.optimization_barrier((residual_rows.astype(jnp.float32) + output_gate * branch_output).astype(jnp.bfloat16))
        return patch_latents(block_out, closing_scale, closing_shift, patch_projection_weight, patch_projection_bias)
    latents = lax.map(finish_rows, jnp.arange(TOKENS // group_rows, dtype=jnp.int32)).reshape(TOKENS, -1)
    pixels = unpatch(latents, TOKENS // LAT_W, LAT_W, LAT_CH)
    padded = jnp.pad(pixels, ((1, 1), (1, 1), (0, 0)))
    return conv_apply(padded, convolution_kernel, convolution_bias)
```

```python
import math

import jax
import jax.numpy as jnp
from jax import lax
from jax.experimental import pallas as pl
from jax.experimental.pallas import tpu as pltpu
from jax.sharding import PartitionSpec as P

HD = 128
WIN = 512
SEQ = 32
TILE = 16
BLOCK = 128
BAND = 2048
FEATS = 2048
WIDTH = 3072
QUARTER = WIDTH // 4
SHARD = WIDTH // TILE
RANKS = 128
DEEP = FEATS + RANKS
EIGHTH = DEEP // 8
KEYS = BLOCK + 2 * WIN

norm_epsilon = 1e-06
latent_scaling = 0.3611
latent_offset = 0.1159

MESH = pl.DeviceIdType.MESH
F32 = jnp.float32
BF16 = jnp.bfloat16


def wait_bytes(ref, sem):
    pltpu.make_async_copy(ref, ref, sem).wait()


def kernel(
    q_hbm,
    k_hbm,
    v_hbm,
    request,
    request_adapter,
    residual_hbm,
    gate,
    weight_hbm,
    down,
    up_hbm,
    scale,
    shift,
    patch_weight,
    patch_bias,
    conv_kernel,
    conv_bias,
    out,
    qbuf,
    kbuf,
    vbuf,
    att,
    wraw,
    wq,
    rbuf,
    mbuf,
    gbuf,
    xbuf,
    msg,
    msgin,
    lat,
    lbuf,
    lfull,
    wc,
    obuf,
    bias_row,
    r_qkv,
    s_qkv,
    r_halo,
    s_halo,
    l_w,
    r_w,
    s_w,
    r_res,
    s_res,
    r_g,
    s_g,
    r_y,
    s_y,
    r_msg,
    s_msg,
    r_lat,
    s_lat,
    r_lh,
    s_lh,
):
    t = lax.axis_index("tile")
    s = lax.axis_index("seq")
    y = t // 4
    z = lax.rem(t, 4)
    core = lax.rem(s, 2)
    x = s // 8
    sibling = s + 1 - 2 * core
    first = s == 0
    last = s == SEQ - 1

    def remote(src, dst, send_sem, recv_sem, where):
        return pltpu.make_async_remote_copy(
            src_ref=src,
            dst_ref=dst,
            send_sem=send_sem,
            recv_sem=recv_sem,
            device_id=where,
            device_id_type=MESH,
        )

    @pl.when(first)
    def _():
        kbuf[0:WIN, :] = jnp.zeros((WIN, HD), BF16)
        vbuf[0:WIN, :] = jnp.zeros((WIN, HD), BF16)
        lbuf[0] = jnp.zeros((48, 128), BF16)

    @pl.when(last)
    def _():
        kbuf[WIN + BAND :, :] = jnp.zeros((WIN, HD), BF16)
        vbuf[WIN + BAND :, :] = jnp.zeros((WIN, HD), BF16)
        lbuf[9] = jnp.zeros((48, 128), BF16)

    @pl.when(t == 0)
    def _():
        lbuf[1:9, 0:16, :] = jnp.zeros((8, 16, 128), BF16)

    @pl.when(t == TILE - 1)
    def _():
        lbuf[1:9, 32:48, :] = jnp.zeros((8, 16, 128), BF16)

    barrier = pltpu.get_barrier_semaphore()

    def greet(d, carry):
        pl.semaphore_signal(
            barrier, inc=1, device_id={"tile": lax.rem(t + d, TILE)}, device_id_type=MESH
        )
        return carry

    lax.fori_loop(1, TILE, greet, 0)
    for d in range(1, 4):
        pl.semaphore_signal(
            barrier, inc=1, device_id={"seq": lax.rem(s + 8 * d, SEQ)}, device_id_type=MESH
        )

    @pl.when(jnp.logical_not(first))
    def _():
        pl.semaphore_signal(barrier, inc=1, device_id={"seq": s - 1}, device_id_type=MESH)

    @pl.when(jnp.logical_not(last))
    def _():
        pl.semaphore_signal(barrier, inc=1, device_id={"seq": s + 1}, device_id_type=MESH)

    w_local = pltpu.make_async_copy(weight_hbm, wraw.at[z, pl.ds(0, FEATS), :], l_w.at[0])
    u_local = pltpu.make_async_copy(up_hbm, wraw.at[z, pl.ds(FEATS, RANKS), :], l_w.at[1])
    w_local.start()
    u_local.start()

    pl.semaphore_wait(
        barrier, TILE - 1 + 3 + jnp.where(first, 0, 1) + jnp.where(last, 0, 1)
    )

    own_rows = pl.ds(pl.multiple_of(WIN + t * BLOCK, BLOCK), BLOCK)
    own_q_rows = pl.ds(pl.multiple_of(t * BLOCK, BLOCK), BLOCK)
    sets = ((k_hbm, kbuf, own_rows), (v_hbm, vbuf, own_rows), (q_hbm, qbuf, own_q_rows))
    for a, (src, dst, rows) in enumerate(sets):

        def send(d, carry, a=a, src=src, dst=dst, rows=rows):
            p = lax.rem(t + d, TILE)
            cols = pl.ds(pl.multiple_of(p * HD, HD), HD)
            remote(
                src.at[:, cols], dst.at[rows, :], s_qkv.at[a], r_qkv.at[a, y], {"tile": p}
            ).start()
            return carry

        lax.fori_loop(1, TILE, send, 0)
        own_cols = pl.ds(pl.multiple_of(t * HD, HD), HD)
        pltpu.make_async_copy(src.at[:, own_cols], dst.at[rows, :], r_qkv.at[a, y]).start()

    adapters = jnp.zeros((1, BLOCK), jnp.int32)
    for r in range(8):
        adapters = adapters + jnp.where(request[...] == r, request_adapter[r], 0)
    owner = lax.broadcasted_iota(jnp.int32, (RANKS, BLOCK), 0) // 32
    kept = jnp.where(jnp.broadcast_to(adapters, (RANKS, BLOCK)) == owner, 1.0, 0.0)
    mbuf[y] = kept.T.astype(BF16)

    for d in range(4):
        y2 = lax.rem(y + d, 4)
        cols = pl.ds(pl.multiple_of(y2 * QUARTER, 128), QUARTER)
        if d == 0:
            pltpu.make_async_copy(residual_hbm.at[:, cols], rbuf.at[y], r_res.at[0]).start()
        else:
            where = {"tile": y2 * 4 + z}
            remote(
                residual_hbm.at[:, cols], rbuf.at[y], s_res.at[0], r_res.at[0], where
            ).start()
            remote(mbuf.at[y], mbuf.at[y], s_res.at[1], r_res.at[1], where).start()

    w_local.wait()
    u_local.wait()
    e_rows = pl.ds(pl.multiple_of((core * 4 + x) * EIGHTH, 16), EIGHTH)
    half_rows = pl.ds(pl.multiple_of(core * 4 * EIGHTH, 16), 4 * EIGHTH)
    for d in range(1, 4):
        z2 = lax.rem(z + d, 4)
        remote(
            wraw.at[z, e_rows, :],
            wraw.at[z, e_rows, :],
            s_w.at[0],
            r_w.at[0],
            {"tile": y * 4 + z2},
        ).start()

    flat_kernel = conv_kernel[...].reshape(144, 512)
    place = lax.broadcasted_iota(jnp.int32, (512, 144), 0)
    tap = lax.broadcasted_iota(jnp.int32, (512, 144), 1)
    lane = lax.rem(place, 128)
    dri = place // 256
    dwi = lax.rem(place // 128, 2)
    pa = lax.rem(lane // 2, 2)
    pb = lax.rem(lane, 2)
    for a in range(2):
        for b in range(2):
            ky = 2 * dri + a + pa - 1
            kx = 2 * dwi + b + pb - 1
            good = (
                (lane < 64)
                & (ky >= 0)
                & (ky < 3)
                & (kx >= 0)
                & (kx < 3)
                & (tap == (ky * 3 + kx) * 16 + lane // 4)
            )
            pick = jnp.where(good, 1.0, 0.0).astype(BF16)
            wc[2 * a + b] = jnp.dot(pick, flat_kernel, preferred_element_type=F32).astype(BF16)
    bias_row[...] = jnp.zeros((8, 128), F32)
    bias_row[0:1, 0:64] = patch_bias[...]

    wait_bytes(wraw.at[pl.ds(0, 3), pl.ds(0, EIGHTH), :], r_w.at[0])
    for d in range(1, 4):
        z2 = lax.rem(z + d, 4)
        for e in range(1, 4):
            remote(
                wraw.at[z2, e_rows, :],
                wraw.at[z2, e_rows, :],
                s_w.at[1],
                r_w.at[1],
                {"seq": lax.rem(s + 8 * e, SEQ)},
            ).start()

    for row in (3, 0):
        for a in range(2):
            buf = (kbuf, vbuf)[a]
            wait_bytes(buf.at[pl.ds(WIN, 4 * BLOCK), :], r_qkv.at[a, row])

    def halo(buf, a, up):
        if up:
            src = buf.at[pl.ds(WIN + 3 * WIN, WIN), :]
            dst = buf.at[pl.ds(0, WIN), :]
            return remote(src, dst, s_halo.at[0], r_halo.at[0], {"seq": s + 1})
        src = buf.at[pl.ds(WIN, WIN), :]
        dst = buf.at[pl.ds(WIN + BAND, WIN), :]
        return remote(src, dst, s_halo.at[1], r_halo.at[1], {"seq": s - 1})

    @pl.when(jnp.logical_not(last))
    def _():
        halo(kbuf, 0, True).start()
        halo(vbuf, 1, True).start()

    @pl.when(jnp.logical_not(first))
    def _():
        halo(kbuf, 0, False).start()
        halo(vbuf, 1, False).start()

    for row in (1, 2):
        for a in range(2):
            buf = (kbuf, vbuf)[a]
            wait_bytes(buf.at[pl.ds(WIN, 4 * BLOCK), :], r_qkv.at[a, row])
    for row in range(4):
        wait_bytes(qbuf.at[pl.ds(0, 4 * BLOCK), :], r_qkv.at[2, row])

    factor = math.log2(math.e) / math.sqrt(HD)
    row_at = lax.broadcasted_iota(jnp.int32, (BLOCK, BLOCK), 0)
    col_at = lax.broadcasted_iota(jnp.int32, (BLOCK, BLOCK), 1)

    def attend(row):
        edge = (first & (row == 0)) | (last & (row == 3))

        def block(b, edged):
            start = pl.multiple_of(row * WIN + b * BLOCK, BLOCK)
            q = qbuf[pl.ds(start, BLOCK), :]
            k = kbuf[pl.ds(start, KEYS), :]
            v = vbuf[pl.ds(start, KEYS), :]
            scores = lax.dot_general(
                q, k, (((1,), (1,)), ((), ())), preferred_element_type=F32
            )
            low = jnp.where(col_at >= row_at, scores[:, :BLOCK], -jnp.inf)
            high = jnp.where(col_at <= row_at, scores[:, KEYS - BLOCK :], -jnp.inf)
            scores = jnp.concatenate([low, scores[:, BLOCK : KEYS - BLOCK], high], axis=1)
            if edged:
                key_at = start + lax.broadcasted_iota(jnp.int32, (BLOCK, KEYS), 1)
                least = jnp.where(first, WIN, 0)
                most = jnp.where(last, WIN + BAND, 2 * WIN + BAND)
                scores = jnp.where((key_at >= least) & (key_at < most), scores, -jnp.inf)
            highest = jnp.max(scores, axis=1, keepdims=True)
            expons = jnp.exp2((scores - highest) * factor)
            totals = jnp.sum(expons, axis=1, keepdims=True)
            weighted = jnp.dot(expons.astype(BF16), v, preferred_element_type=F32)
            att[row, b] = (weighted / totals).astype(BF16)

        @pl.when(edge)
        def _():
            for b in range(4):
                block(b, True)

        @pl.when(jnp.logical_not(edge))
        def _():
            for b in range(4):
                block(b, False)

    head_cols = pl.ds(pl.multiple_of(t * HD, HD), HD)

    def send_heads(row):
        pltpu.make_async_copy(
            att.at[row, z], gbuf.at[row, :, head_cols], r_g.at[row]
        ).start()
        for d in range(1, 4):
            z2 = lax.rem(z + d, 4)
            remote(
                att.at[row, z2],
                gbuf.at[row, :, head_cols],
                s_g.at[0],
                r_g.at[row],
                {"tile": y * 4 + z2},
            ).start()

    y_up = {"tile": lax.rem(y + 1, 4) * 4 + z}
    y_down = {"tile": lax.rem(y + 3, 4) * 4 + z}

    def group_cols(which, offset=0, width=512):
        at = lax.rem(y + which, 4) * 512 + offset
        return pl.ds(pl.multiple_of(at, 128), width)

    def send_group(row):
        cols = group_cols(0)
        wait_bytes(gbuf.at[row, :, pl.ds(0, 512)], r_g.at[row])
        ref = gbuf.at[row, :, cols]
        remote(ref, ref, s_y.at[0], r_y.at[0, row], y_up).start()
        remote(ref, ref, s_y.at[0], r_y.at[1, row], y_down).start()

    def pass_on(row):
        wait_bytes(gbuf.at[row, :, pl.ds(0, 512)], r_y.at[0, row])
        ref = gbuf.at[row, :, group_cols(3, 0, 256)]
        remote(ref, ref, s_y.at[1], r_y.at[2, row], y_up).start()
        wait_bytes(gbuf.at[row, :, pl.ds(0, 512)], r_y.at[1, row])
        ref = gbuf.at[row, :, group_cols(1, 256, 256)]
        remote(ref, ref, s_y.at[1], r_y.at[3, row], y_down).start()

    row_a = jnp.where(core == 0, 3, 0)
    row_b = 3 - row_a

    def wait_halo(row):
        missing = (first & (row == 0)) | (last & (row == 3))

        @pl.when(jnp.logical_not(missing))
        def _():
            wait_bytes(kbuf.at[pl.ds(0, 2 * WIN), :], r_halo.at[jnp.where(row == 0, 0, 1)])

    attend(1)
    send_heads(1)
    attend(2)
    send_heads(2)
    send_group(1)
    wait_halo(row_a)
    attend(row_a)
    send_heads(row_a)
    send_group(2)

    wait_bytes(wraw.at[pl.ds(0, 3), pl.ds(0, 3 * EIGHTH), :], r_w.at[1])
    for d in range(1, 4):
        z2 = lax.rem(z + d, 4)
        ref = wraw.at[z2, half_rows, :]
        remote(ref, ref, s_w.at[2], r_w.at[2], {"seq": sibling}).start()

    wait_halo(row_b)
    attend(row_b)
    send_heads(row_b)
    send_group(row_a)
    pass_on(1)
    send_group(row_b)
    pass_on(2)

    wait_bytes(wraw.at[pl.ds(0, 3), pl.ds(0, 4 * EIGHTH), :], r_w.at[2])
    for c in range(DEEP // 272):
        rows = pl.ds(c * 272, 272)
        wq[rows, :] = jnp.concatenate([wraw[i, rows, :] for i in range(4)], axis=1)

    quarter = pl.ds(pl.multiple_of(y * QUARTER, 128), QUARTER)
    spread = jnp.where(
        lax.broadcasted_iota(jnp.int32, (64, 128), 0)
        == lax.broadcasted_iota(jnp.int32, (64, 128), 1),
        1.0,
        0.0,
    ).astype(BF16)
    patch_rows = pl.ds(pl.multiple_of(y * QUARTER, 128), QUARTER)
    patch = jnp.dot(patch_weight[patch_rows, :], spread, preferred_element_type=F32)
    gain = 1.0 + scale[:, quarter]
    which = lax.broadcasted_iota(jnp.int32, (8, QUARTER), 0)
    pair = jnp.where(which == 0, gain, jnp.where(which == 1, shift[:, quarter], 0.0))
    sums = jnp.dot(pair, patch, precision=lax.Precision.HIGHEST, preferred_element_type=F32)
    patch = patch.astype(BF16)

    pass_on(row_a)
    pass_on(row_b)
    for row in range(4):
        wait_bytes(gbuf.at[row, :, pl.ds(0, 256)], r_y.at[2, row])
        wait_bytes(gbuf.at[row, :, pl.ds(0, 256)], r_y.at[3, row])
    wait_bytes(rbuf, r_res.at[0])
    wait_bytes(mbuf.at[pl.ds(0, 3)], r_res.at[1])

    heads = gbuf[:, :, pl.ds(0, FEATS)].reshape(512, FEATS)
    lowered = jnp.dot(heads, down[...], preferred_element_type=F32)
    lowered = jnp.where(mbuf[...].reshape(512, RANKS) > 0, lowered, 0.0).astype(BF16)
    gbuf[:, :, pl.ds(FEATS, RANKS)] = lowered.reshape(4, BLOCK, RANKS)
    total = jnp.zeros((512, 1), F32)
    for n in range(3):
        cols = pl.ds(n * 256, 256)
        gate_cols = pl.ds(pl.multiple_of(y * QUARTER + n * 256, 128), 256)
        branch = jnp.dot(
            gbuf[...].reshape(512, DEEP), wq[:, cols], preferred_element_type=F32
        )
        base = rbuf[:, :, cols].reshape(512, 256).astype(F32)
        value = (base + gate[:, gate_cols] * branch).astype(BF16).astype(F32)
        xbuf[:, cols] = value
        total = total + jnp.sum(value, axis=1, keepdims=True)
    average = total * (1.0 / QUARTER)
    centered = xbuf[...] - average
    squares = jnp.sum(centered * centered, axis=1, keepdims=True)
    part = jnp.dot((centered * gain).astype(BF16), patch, preferred_element_type=F32)
    lane_at = lax.broadcasted_iota(jnp.int32, (512, 128), 1)
    part = jnp.where(lane_at == 64, average, jnp.where(lane_at == 65, squares, part))
    for row in range(4):
        msg[row, 0:BLOCK, :] = part[row * BLOCK : (row + 1) * BLOCK]
        msg[row, BLOCK : BLOCK + 8, :] = sums
    pltpu.make_async_copy(msg.at[y], msgin.at[y], r_msg.at[0]).start()
    for d in range(1, 4):
        y2 = lax.rem(y + d, 4)
        remote(
            msg.at[y2], msgin.at[y], s_msg.at[0], r_msg.at[0], {"tile": y2 * 4 + z}
        ).start()
    wait_bytes(msgin, r_msg.at[0])

    means = [msgin[i, 0:BLOCK, 64:65] for i in range(4)]
    spreads = [msgin[i, 0:BLOCK, 65:66] for i in range(4)]
    overall = (means[0] + means[1] + means[2] + means[3]) * 0.25
    variance = spreads[0] + spreads[1] + spreads[2] + spreads[3]
    projected = jnp.zeros((BLOCK, 128), F32)
    constant = bias_row[0:1, :]
    for i in range(4):
        off = means[i] - overall
        variance = variance + QUARTER * off * off
        projected = projected + (
            msgin[i, 0:BLOCK, :] + off * msgin[i, BLOCK : BLOCK + 1, :]
        )
        constant = constant + msgin[i, BLOCK + 1 : BLOCK + 2, :]
    projected = projected * lax.rsqrt(variance * (1.0 / WIDTH) + norm_epsilon) + constant
    latents = projected / latent_scaling + latent_offset
    small = lax.broadcasted_iota(jnp.int32, (BLOCK, 128), 1) < 64
    lat[...] = jnp.where(small, latents, 0.0).astype(BF16)

    half = lax.rem(t, 2)
    line = t // 2 + 1

    def hand(i, target, src, dst):
        far = remote(src, dst, s_lat.at[i], r_lat.at[0], {"tile": target})
        near = pltpu.make_async_copy(src, dst, r_lat.at[0])

        @pl.when(target != t)
        def _():
            far.start()

        @pl.when(target == t)
        def _():
            near.start()

        def finish():
            @pl.when(target != t)
            def _():
                far.wait_send()

        return finish

    finishes = []
    for i in range(8):
        begin = max(0, i - 1) * 16
        end = min(8, i + 2) * 16
        off = 16 if i == 0 else 0
        finishes.append(
            hand(
                i,
                half * 8 + i,
                lat.at[pl.ds(begin, end - begin), :],
                lbuf.at[line, pl.ds(off, end - begin), :],
            )
        )
    cross_src = pl.ds(pl.multiple_of(112 * (1 - half), 16), 16)
    cross_dst = pl.ds(pl.multiple_of(32 * half, 16), 16)
    finishes.append(
        hand(8, 8 - half, lat.at[cross_src, :], lbuf.at[line, cross_dst, :])
    )
    side = (t == 0) | (t == TILE - 1)

    @pl.when(side)
    def _():
        wait_bytes(lbuf.at[pl.ds(1, 8), pl.ds(0, 32), :], r_lat.at[0])

    @pl.when(jnp.logical_not(side))
    def _():
        wait_bytes(lbuf.at[pl.ds(1, 8), :, :], r_lat.at[0])

    to_next = remote(lbuf.at[8], lbuf.at[0], s_lh.at[0], r_lh.at[0], {"seq": s + 1})
    to_prev = remote(lbuf.at[1], lbuf.at[9], s_lh.at[1], r_lh.at[1], {"seq": s - 1})

    @pl.when(jnp.logical_not(last))
    def _():
        to_next.start()

    @pl.when(jnp.logical_not(first))
    def _():
        to_prev.start()

    @pl.when(jnp.logical_not(first))
    def _():
        wait_bytes(lbuf.at[0], r_lh.at[0])

    @pl.when(jnp.logical_not(last))
    def _():
        wait_bytes(lbuf.at[9], r_lh.at[1])

    lfull[...] = lbuf[...].astype(F32)
    columns = [lfull[:, 15 + i : 31 + i, :].astype(BF16) for i in range(3)]
    for a in range(2):
        for b in range(2):
            near = jnp.concatenate(
                [
                    columns[j + b][i + a : i + a + 8].reshape(128, 128)
                    for i in range(2)
                    for j in range(2)
                ],
                axis=1,
            )
            value = (
                jnp.dot(near, wc[2 * a + b], preferred_element_type=F32) + conv_bias[...]
            ).reshape(8, 16, 512)
            for r in range(8):
                for c in range(4):
                    obuf[c, 2 * r + a, pl.ds(b, 16, stride=2), :] = value[
                        r, :, c * 128 : (c + 1) * 128
                    ]
    for c in range(4):
        out[:, :, c * 128 : (c + 1) * 128] = obuf[c].astype(BF16)

    for a in range(3):
        wait_bytes(kbuf.at[pl.ds(0, 15 * BLOCK), :], s_qkv.at[a])

    @pl.when(jnp.logical_not(last))
    def _():
        wait_bytes(kbuf.at[pl.ds(0, 2 * WIN), :], s_halo.at[0])
        to_next.wait_send()

    @pl.when(jnp.logical_not(first))
    def _():
        wait_bytes(kbuf.at[pl.ds(0, 2 * WIN), :], s_halo.at[1])
        to_prev.wait_send()

    wait_bytes(wraw.at[pl.ds(0, 3), pl.ds(0, EIGHTH), :], s_w.at[0])
    wait_bytes(wraw.at[pl.ds(0, 3), pl.ds(0, 3 * EIGHTH), :], s_w.at[1])
    wait_bytes(wraw.at[pl.ds(0, 3), pl.ds(0, 4 * EIGHTH), :], s_w.at[2])
    wait_bytes(rbuf.at[pl.ds(0, 3)], s_res.at[0])
    wait_bytes(mbuf.at[pl.ds(0, 3)], s_res.at[1])
    wait_bytes(att.at[pl.ds(0, 3)], s_g.at[0])
    wait_bytes(gbuf.at[:, :, pl.ds(0, 1024)], s_y.at[0])
    wait_bytes(gbuf.at[:, :, pl.ds(0, 512)], s_y.at[1])
    wait_bytes(msg.at[pl.ds(0, 3)], s_msg.at[0])
    for finish in finishes:
        finish()


def on_device(
    queries,
    head_keys,
    head_values,
    region_request,
    request_adapter,
    residual,
    output_gate,
    output_weight,
    adapter_down_factors,
    adapter_up_factors,
    closing_scale,
    closing_shift,
    patch_projection_weight,
    patch_projection_bias,
    convolution_kernel,
    convolution_bias,
):
    far = pl.BlockSpec(memory_space=pl.ANY)
    near = pl.BlockSpec(memory_space=pltpu.VMEM)
    scalars = pl.BlockSpec(memory_space=pltpu.SMEM)
    dma = pltpu.SemaphoreType.DMA
    return pl.pallas_call(
        kernel,
        out_shape=jax.ShapeDtypeStruct((16, 32, 512), BF16),
        in_specs=[
            far, far, far, near, scalars, far, near, far,
            near, far, near, near, near, near, near, near,
        ],
        out_specs=near,
        scratch_shapes=[
            pltpu.VMEM((BAND, HD), BF16),
            pltpu.VMEM((BAND + 2 * WIN, HD), BF16),
            pltpu.VMEM((BAND + 2 * WIN, HD), BF16),
            pltpu.VMEM((4, 4, BLOCK, HD), BF16),
            pltpu.VMEM((4, DEEP, SHARD), BF16),
            pltpu.VMEM((DEEP, QUARTER), BF16),
            pltpu.VMEM((4, BLOCK, QUARTER), BF16),
            pltpu.VMEM((4, BLOCK, RANKS), BF16),
            pltpu.VMEM((4, BLOCK, DEEP), BF16),
            pltpu.VMEM((512, QUARTER), F32),
            pltpu.VMEM((4, BLOCK + 8, 128), F32),
            pltpu.VMEM((4, BLOCK + 8, 128), F32),
            pltpu.VMEM((BLOCK, 128), BF16),
            pltpu.VMEM((10, 48, 128), BF16),
            pltpu.VMEM((10, 48, 128), F32),
            pltpu.VMEM((4, 512, 512), BF16),
            pltpu.VMEM((4, 16, 32, 128), F32),
            pltpu.VMEM((8, 128), F32),
            dma((3, 4)),
            dma((3,)),
            dma((2,)),
            dma((2,)),
            dma((2,)),
            dma((3,)),
            dma((3,)),
            dma((2,)),
            dma((2,)),
            dma((4,)),
            dma((1,)),
            dma((4, 4)),
            dma((2,)),
            dma((1,)),
            dma((1,)),
            dma((1,)),
            dma((9,)),
            dma((2,)),
            dma((2,)),
        ],
        compiler_params=pltpu.CompilerParams(
            collective_id=0, has_side_effects=True, vmem_limit_bytes=48 * 1024 * 1024
        ),
    )(
        queries,
        head_keys,
        head_values,
        region_request.reshape(1, -1),
        request_adapter,
        residual,
        output_gate.reshape(1, -1),
        output_weight,
        adapter_down_factors,
        adapter_up_factors,
        closing_scale.reshape(1, -1),
        closing_shift.reshape(1, -1),
        patch_projection_weight,
        patch_projection_bias.reshape(1, -1),
        convolution_kernel,
        convolution_bias.reshape(1, -1),
    )


def solution(mesh):
    return jax.shard_map(
        on_device,
        mesh=mesh,
        in_specs=(
            P(("seq", "tile"), None),
            P(("seq", "tile"), None),
            P(("seq", "tile"), None),
            P(("seq", "tile")),
            P(),
            P(("seq", "tile"), None),
            P(),
            P(None, "tile"),
            P(),
            P(None, "tile"),
            P(),
            P(),
            P(),
            P(),
            P(),
            P(),
        ),
        out_specs=P("seq", "tile", None),
        check_vma=False,
    )
```

```python
import math

import jax
import jax.numpy as jnp
from jax import lax
from jax.experimental import pallas as pl
from jax.experimental.pallas import tpu as pltpu
from jax.sharding import PartitionSpec as P

HD = 128
WIN = 512
SEQ = 32
TILE = 16
BLOCK = 128
BAND = 2048
FEATS = 2048
WIDTH = 3072
QUARTER = WIDTH // 4
SHARD = WIDTH // TILE
RANKS = 128
DEEP = FEATS + RANKS
PAD_DEEP = 2304
PIECE = SHARD // 4
HALF = PAD_DEEP // 2
KEYS = BLOCK + 2 * WIN

norm_epsilon = 1e-06
latent_scaling = 0.3611
latent_offset = 0.1159

MESH = pl.DeviceIdType.MESH
F32 = jnp.float32
BF16 = jnp.bfloat16


def wait_bytes(ref, sem):
    pltpu.make_async_copy(ref, ref, sem).wait()


def kernel(
    q_hbm,
    k_hbm,
    v_hbm,
    request,
    request_adapter,
    residual_hbm,
    gate,
    weight_hbm,
    down,
    up_hbm,
    scale,
    shift,
    patch_weight,
    patch_bias,
    conv_kernel,
    conv_bias,
    out,
    qbuf,
    kbuf,
    vbuf,
    att,
    wq,
    patch_wide,
    rbuf,
    mbuf,
    gbuf,
    xbuf,
    msg,
    msgin,
    lat,
    lbuf,
    lfull,
    wc,
    obuf,
    bias_row,
    r_qkv,
    s_qkv,
    r_halo,
    s_halo,
    l_w,
    r_w,
    s_w,
    r_res,
    s_res,
    r_g,
    s_g,
    r_y,
    s_y,
    r_msg,
    s_msg,
    r_lat,
    s_lat,
):
    t = lax.axis_index("tile")
    s = lax.axis_index("seq")
    y = t // 4
    z = lax.rem(t, 4)
    core = lax.rem(s, 2)
    x = s // 8
    sibling = s + 1 - 2 * core
    first = s == 0
    last = s == SEQ - 1

    def remote(src, dst, send_sem, recv_sem, where):
        return pltpu.make_async_remote_copy(
            src_ref=src,
            dst_ref=dst,
            send_sem=send_sem,
            recv_sem=recv_sem,
            device_id=where,
            device_id_type=MESH,
        )

    @pl.when(first)
    def _():
        kbuf[0:WIN, :] = jnp.zeros((WIN, HD), BF16)
        vbuf[0:WIN, :] = jnp.zeros((WIN, HD), BF16)
        lbuf[0] = jnp.zeros((48, 128), BF16)

    @pl.when(last)
    def _():
        kbuf[WIN + BAND :, :] = jnp.zeros((WIN, HD), BF16)
        vbuf[WIN + BAND :, :] = jnp.zeros((WIN, HD), BF16)
        lbuf[9] = jnp.zeros((48, 128), BF16)

    @pl.when(t == 0)
    def _():
        lbuf[:, 0:16, :] = jnp.zeros((10, 16, 128), BF16)

    @pl.when(t == TILE - 1)
    def _():
        lbuf[:, 32:48, :] = jnp.zeros((10, 16, 128), BF16)

    wq[:, DEEP:] = jnp.zeros((QUARTER, PAD_DEEP - DEEP), BF16)

    barrier = pltpu.get_barrier_semaphore()

    def greet(d, carry):
        pl.semaphore_signal(
            barrier, inc=1, device_id={"tile": lax.rem(t + d, TILE)}, device_id_type=MESH
        )
        return carry

    lax.fori_loop(1, TILE, greet, 0)
    for d in range(1, 4):
        pl.semaphore_signal(
            barrier, inc=1, device_id={"seq": lax.rem(s + 8 * d, SEQ)}, device_id_type=MESH
        )

    def ring(d):
        far = lax.rem(lax.rem(s // 2, 4) * 4 + z + d + 16, 16)
        return {"seq": (x * 4 + far // 4) * 2 + core, "tile": y * 4 + lax.rem(far, 4)}

    two = 2 - 4 * core
    for d in (1, -1, -two):
        pl.semaphore_signal(barrier, inc=1, device_id=ring(d), device_id_type=MESH)

    @pl.when(jnp.logical_not(first))
    def _():
        pl.semaphore_signal(barrier, inc=1, device_id={"seq": s - 1}, device_id_type=MESH)
        for p in (14, 15):
            pl.semaphore_signal(
                barrier, inc=1, device_id={"seq": s - 1, "tile": p}, device_id_type=MESH
            )

    @pl.when(jnp.logical_not(last))
    def _():
        pl.semaphore_signal(barrier, inc=1, device_id={"seq": s + 1}, device_id_type=MESH)
        for p in (0, 1):
            pl.semaphore_signal(
                barrier, inc=1, device_id={"seq": s + 1, "tile": p}, device_id_type=MESH
            )

    bottom = (t >= TILE - 2) & jnp.logical_not(last)
    top = (t <= 1) & jnp.logical_not(first)

    own_shard = pl.ds(pl.multiple_of(z * SHARD, 64), SHARD)
    w_local = pltpu.make_async_copy(weight_hbm, wq.at[own_shard, pl.ds(0, FEATS)], l_w.at[0])
    u_local = pltpu.make_async_copy(up_hbm, wq.at[own_shard, pl.ds(FEATS, RANKS)], l_w.at[1])
    w_local.start()
    u_local.start()

    pl.semaphore_wait(
        barrier,
        TILE
        + 5
        + jnp.where(first, 0, 1)
        + jnp.where(last, 0, 1)
        + jnp.where(bottom, TILE, 0)
        + jnp.where(top, TILE, 0),
    )

    half_cols = pl.ds(pl.multiple_of(core * HALF, 128), HALF)

    def piece(z2):
        return wq.at[pl.ds(pl.multiple_of(z2 * SHARD + x * PIECE, 16), PIECE), half_cols]

    w_local.wait()
    u_local.wait()
    for d in (1, -1, two):
        remote(piece(z), piece(z), s_w.at[0], r_w.at[0], ring(d)).start()

    own_rows = pl.ds(pl.multiple_of(WIN + t * BLOCK, BLOCK), BLOCK)
    own_q_rows = pl.ds(pl.multiple_of(t * BLOCK, BLOCK), BLOCK)
    sets = ((k_hbm, kbuf, own_rows), (v_hbm, vbuf, own_rows), (q_hbm, qbuf, own_q_rows))
    for a, (src, dst, rows) in enumerate(sets):

        def send(d, carry, a=a, src=src, dst=dst, rows=rows):
            p = lax.rem(t + d, TILE)
            cols = pl.ds(pl.multiple_of(p * HD, HD), HD)
            remote(
                src.at[:, cols], dst.at[rows, :], s_qkv.at[a], r_qkv.at[a, y], {"tile": p}
            ).start()
            return carry

        lax.fori_loop(1, TILE, send, 0)
        own_cols = pl.ds(pl.multiple_of(t * HD, HD), HD)
        pltpu.make_async_copy(src.at[:, own_cols], dst.at[rows, :], r_qkv.at[a, y]).start()

    adapters = jnp.zeros((1, BLOCK), jnp.int32)
    for r in range(8):
        adapters = adapters + jnp.where(request[...] == r, request_adapter[r], 0)
    owner = lax.broadcasted_iota(jnp.int32, (RANKS, BLOCK), 0) // 32
    kept = jnp.where(jnp.broadcast_to(adapters, (RANKS, BLOCK)) == owner, 1.0, 0.0)
    mbuf[y] = kept.T.astype(BF16)

    for d in range(4):
        y2 = lax.rem(y + d, 4)
        cols = pl.ds(pl.multiple_of(y2 * QUARTER, 128), QUARTER)
        if d == 0:
            pltpu.make_async_copy(residual_hbm.at[:, cols], rbuf.at[y], r_res.at[0]).start()
        else:
            where = {"tile": y2 * 4 + z}
            remote(
                residual_hbm.at[:, cols], rbuf.at[y], s_res.at[0], r_res.at[0], where
            ).start()
            remote(mbuf.at[y], mbuf.at[y], s_res.at[1], r_res.at[1], where).start()

    wait_bytes(wq.at[pl.ds(0, 3 * PIECE), pl.ds(0, HALF)], r_w.at[0])
    for d in range(1, 4):
        ref = piece(lax.rem(z + d, 4))
        for e in range(1, 4):
            remote(
                ref, ref, s_w.at[1], r_w.at[1], {"seq": lax.rem(s + 8 * e, SEQ)}
            ).start()

    flat_kernel = conv_kernel[...].reshape(144, 512)
    place = lax.broadcasted_iota(jnp.int32, (512, 144), 0)
    tap = lax.broadcasted_iota(jnp.int32, (512, 144), 1)
    lane = lax.rem(place, 128)
    dri = place // 256
    dwi = lax.rem(place // 128, 2)
    pa = lax.rem(lane // 2, 2)
    pb = lax.rem(lane, 2)
    for a in range(2):
        for b in range(2):
            ky = 2 * dri + a + pa - 1
            kx = 2 * dwi + b + pb - 1
            good = (
                (lane < 64)
                & (ky >= 0)
                & (ky < 3)
                & (kx >= 0)
                & (kx < 3)
                & (tap == (ky * 3 + kx) * 16 + lane // 4)
            )
            pick = jnp.where(good, 1.0, 0.0).astype(BF16)
            wc[2 * a + b] = jnp.dot(pick, flat_kernel, preferred_element_type=F32).astype(BF16)
    bias_row[...] = jnp.zeros((8, 128), F32)
    bias_row[0:1, 0:64] = patch_bias[...]

    quarter = pl.ds(pl.multiple_of(y * QUARTER, 128), QUARTER)
    patch_wide[0:64, :] = patch_weight[:, quarter]
    patch_wide[64:128, :] = jnp.zeros((64, QUARTER), BF16)
    across = (((1,), (1,)), ((), ()))
    gain = 1.0 + scale[:, quarter]
    which = lax.broadcasted_iota(jnp.int32, (8, QUARTER), 0)
    pair = jnp.where(which == 0, gain, jnp.where(which == 1, shift[:, quarter], 0.0))
    sums = lax.dot_general(
        pair,
        patch_wide[...].astype(F32),
        across,
        precision=lax.Precision.HIGHEST,
        preferred_element_type=F32,
    )

    wait_bytes(wq.at[pl.ds(0, 9 * PIECE), pl.ds(0, HALF)], r_w.at[1])
    for d in range(1, 4):
        z2 = lax.rem(z + d, 4)
        ref = wq.at[pl.ds(pl.multiple_of(z2 * SHARD, 64), SHARD), half_cols]
        remote(ref, ref, s_w.at[2], r_w.at[2], {"seq": sibling}).start()

    for row in (3, 0):
        for a in range(2):
            buf = (kbuf, vbuf)[a]
            wait_bytes(buf.at[pl.ds(WIN, 4 * BLOCK), :], r_qkv.at[a, row])

    def halo(buf, a, up):
        if up:
            src = buf.at[pl.ds(WIN + 3 * WIN, WIN), :]
            dst = buf.at[pl.ds(0, WIN), :]
            return remote(src, dst, s_halo.at[0], r_halo.at[0], {"seq": s + 1})
        src = buf.at[pl.ds(WIN, WIN), :]
        dst = buf.at[pl.ds(WIN + BAND, WIN), :]
        return remote(src, dst, s_halo.at[1], r_halo.at[1], {"seq": s - 1})

    @pl.when(jnp.logical_not(last))
    def _():
        halo(kbuf, 0, True).start()
        halo(vbuf, 1, True).start()

    @pl.when(jnp.logical_not(first))
    def _():
        halo(kbuf, 0, False).start()
        halo(vbuf, 1, False).start()

    for row in (1, 2):
        for a in range(2):
            buf = (kbuf, vbuf)[a]
            wait_bytes(buf.at[pl.ds(WIN, 4 * BLOCK), :], r_qkv.at[a, row])
    for row in range(4):
        wait_bytes(qbuf.at[pl.ds(0, 4 * BLOCK), :], r_qkv.at[2, row])

    factor = math.log2(math.e) / math.sqrt(HD)
    row_at = lax.broadcasted_iota(jnp.int32, (BLOCK, BLOCK), 0)
    col_at = lax.broadcasted_iota(jnp.int32, (BLOCK, BLOCK), 1)

    def attend(row):
        edge = (first & (row == 0)) | (last & (row == 3))

        def block(b, edged):
            start = pl.multiple_of(row * WIN + b * BLOCK, BLOCK)
            q = qbuf[pl.ds(start, BLOCK), :]
            k = kbuf[pl.ds(start, KEYS), :]
            v = vbuf[pl.ds(start, KEYS), :]
            scores = lax.dot_general(
                q, k, (((1,), (1,)), ((), ())), preferred_element_type=F32
            )
            low = jnp.where(col_at >= row_at, scores[:, :BLOCK], -jnp.inf)
            high = jnp.where(col_at <= row_at, scores[:, KEYS - BLOCK :], -jnp.inf)
            scores = jnp.concatenate([low, scores[:, BLOCK : KEYS - BLOCK], high], axis=1)
            if edged:
                key_at = start + lax.broadcasted_iota(jnp.int32, (BLOCK, KEYS), 1)
                least = jnp.where(first, WIN, 0)
                most = jnp.where(last, WIN + BAND, 2 * WIN + BAND)
                scores = jnp.where((key_at >= least) & (key_at < most), scores, -jnp.inf)
            highest = jnp.max(scores, axis=1, keepdims=True)
            expons = jnp.exp2((scores - highest) * factor)
            totals = jnp.sum(expons, axis=1, keepdims=True)
            weighted = jnp.dot(expons.astype(BF16), v, preferred_element_type=F32)
            att[row, b] = (weighted / totals).astype(BF16)

        @pl.when(edge)
        def _():
            for b in range(4):
                block(b, True)

        @pl.when(jnp.logical_not(edge))
        def _():
            for b in range(4):
                block(b, False)

    head_cols = pl.ds(pl.multiple_of(t * HD, HD), HD)

    def send_heads(row):
        pltpu.make_async_copy(
            att.at[row, z], gbuf.at[row, :, head_cols], r_g.at[row]
        ).start()
        for d in range(1, 4):
            z2 = lax.rem(z + d, 4)
            remote(
                att.at[row, z2],
                gbuf.at[row, :, head_cols],
                s_g.at[0],
                r_g.at[row],
                {"tile": y * 4 + z2},
            ).start()

    def send_group(row):
        wait_bytes(gbuf.at[row, :, pl.ds(0, 512)], r_g.at[row])
        ref = gbuf.at[row, :, pl.ds(pl.multiple_of(y * 512, 128), 512)]
        for d in range(1, 4):
            where = {"tile": lax.rem(y + d, 4) * 4 + z}
            remote(ref, ref, s_y.at[0], r_y.at[row], where).start()

    row_a = jnp.where(core == 0, 3, 0)
    row_b = 3 - row_a

    def wait_halo(row):
        missing = (first & (row == 0)) | (last & (row == 3))

        @pl.when(jnp.logical_not(missing))
        def _():
            wait_bytes(kbuf.at[pl.ds(0, 2 * WIN), :], r_halo.at[jnp.where(row == 0, 0, 1)])

    def project(row):
        wait_bytes(gbuf.at[row, :, pl.ds(0, 3 * 512)], r_y.at[row])
        lowered = jnp.dot(gbuf[row, :, pl.ds(0, FEATS)], down[...], preferred_element_type=F32)
        lowered = jnp.where(mbuf[row] > 0, lowered, 0.0).astype(BF16)
        gbuf[row, :, pl.ds(FEATS, RANKS)] = lowered
        total = jnp.zeros((BLOCK, 1), F32)
        for n in range(3):
            cols = pl.ds(n * 256, 256)
            gate_cols = pl.ds(pl.multiple_of(y * QUARTER + n * 256, 128), 256)
            branch = lax.dot_general(
                gbuf[row],
                wq[pl.ds(n * 256, 256), pl.ds(0, DEEP)],
                across,
                preferred_element_type=F32,
            )
            base = rbuf[row, :, cols].astype(F32)
            value = (base + gate[:, gate_cols] * branch).astype(BF16).astype(F32)
            xbuf[:, cols] = value
            total = total + jnp.sum(value, axis=1, keepdims=True)
        average = total * (1.0 / QUARTER)
        centered = xbuf[...] - average
        squares = jnp.sum(centered * centered, axis=1, keepdims=True)
        part = lax.dot_general(
            (centered * gain).astype(BF16), patch_wide[...], across, preferred_element_type=F32
        )
        lane_at = lax.broadcasted_iota(jnp.int32, (BLOCK, 128), 1)
        part = jnp.where(lane_at == 64, average, jnp.where(lane_at == 65, squares, part))
        msg[row, 0:BLOCK, :] = part
        msg[row, BLOCK : BLOCK + 8, :] = sums

        @pl.when(row == y)
        def _():
            pltpu.make_async_copy(msg.at[row], msgin.at[y], r_msg.at[0]).start()

        @pl.when(row != y)
        def _():
            where = {"tile": row * 4 + z}
            remote(msg.at[row], msgin.at[y], s_msg.at[0], r_msg.at[0], where).start()

    attend(1)
    send_heads(1)
    attend(2)
    send_heads(2)
    send_group(1)
    wait_halo(row_a)
    attend(row_a)
    send_heads(row_a)
    send_group(2)
    wait_bytes(wq.at[pl.ds(0, 3 * SHARD), pl.ds(0, HALF)], r_w.at[2])
    wait_bytes(rbuf, r_res.at[0])
    wait_bytes(mbuf.at[pl.ds(0, 3)], r_res.at[1])
    project(1)
    send_group(row_a)
    wait_halo(row_b)
    attend(row_b)
    send_heads(row_b)
    project(2)
    send_group(row_b)
    project(row_a)
    project(row_b)
    wait_bytes(msgin, r_msg.at[0])

    means = [msgin[i, 0:BLOCK, 64:65] for i in range(4)]
    spreads = [msgin[i, 0:BLOCK, 65:66] for i in range(4)]
    overall = (means[0] + means[1] + means[2] + means[3]) * 0.25
    variance = spreads[0] + spreads[1] + spreads[2] + spreads[3]
    projected = jnp.zeros((BLOCK, 128), F32)
    constant = bias_row[0:1, :]
    for i in range(4):
        off = means[i] - overall
        variance = variance + QUARTER * off * off
        projected = projected + (
            msgin[i, 0:BLOCK, :] + off * msgin[i, BLOCK : BLOCK + 1, :]
        )
        constant = constant + msgin[i, BLOCK + 1 : BLOCK + 2, :]
    projected = projected * lax.rsqrt(variance * (1.0 / WIDTH) + norm_epsilon) + constant
    latents = projected / latent_scaling + latent_offset
    small = lax.broadcasted_iota(jnp.int32, (BLOCK, 128), 1) < 64
    lat[...] = jnp.where(small, latents, 0.0).astype(BF16)

    half = lax.rem(t, 2)
    line = t // 2 + 1

    def hand(i, target, src, dst, shift, sending):
        recv = r_lat.at[shift % 3]
        if shift == 0:
            far = remote(src, dst, s_lat.at[i], recv, {"tile": target})
            near = pltpu.make_async_copy(src, dst, recv)
            away = target != t

            @pl.when(target == t)
            def _():
                near.start()
        else:
            where = {"seq": s + shift, "tile": target}
            far = remote(src, dst, s_lat.at[i], recv, where)
            away = sending

        @pl.when(away)
        def _():
            far.start()

        def finish():
            @pl.when(away)
            def _():
                far.wait_send()

        return finish

    finishes = []
    cross_src = pl.ds(pl.multiple_of(112 * (1 - half), 16), 16)
    cross_dst = pl.ds(pl.multiple_of(32 * half, 16), 16)
    for k, (shift, sending, at) in enumerate(((1, bottom, 0), (-1, top, 9), (0, None, line))):
        for i in range(8):
            begin = max(0, i - 1) * 16
            size = min(8, i + 2) * 16 - begin
            src = lat.at[pl.ds(begin, size), :]
            dst = lbuf.at[at, pl.ds(16 if i == 0 else 0, size), :]
            finishes.append(hand(9 * k + i, half * 8 + i, src, dst, shift, sending))
        src = lat.at[cross_src, :]
        dst = lbuf.at[at, cross_dst, :]
        finishes.append(hand(9 * k + 8, 8 - half, src, dst, shift, sending))
    side = (t == 0) | (t == TILE - 1)

    def wait_lines(begin, count, sem):
        @pl.when(side)
        def _():
            wait_bytes(lbuf.at[pl.ds(begin, count), pl.ds(0, 32), :], sem)

        @pl.when(jnp.logical_not(side))
        def _():
            wait_bytes(lbuf.at[pl.ds(begin, count), :, :], sem)

    wait_lines(1, 8, r_lat.at[0])

    @pl.when(jnp.logical_not(first))
    def _():
        wait_lines(0, 1, r_lat.at[1])

    @pl.when(jnp.logical_not(last))
    def _():
        wait_lines(9, 1, r_lat.at[2])

    lfull[...] = lbuf[...].astype(F32)
    columns = [lfull[:, 15 + i : 31 + i, :].astype(BF16) for i in range(3)]
    for a in range(2):
        for b in range(2):
            near = jnp.concatenate(
                [
                    columns[j + b][i + a : i + a + 8].reshape(128, 128)
                    for i in range(2)
                    for j in range(2)
                ],
                axis=1,
            )
            value = (
                jnp.dot(near, wc[2 * a + b], preferred_element_type=F32) + conv_bias[...]
            ).reshape(8, 16, 512)
            for r in range(8):
                for c in range(4):
                    obuf[c, 2 * r + a, pl.ds(b, 16, stride=2), :] = value[
                        r, :, c * 128 : (c + 1) * 128
                    ]
    for c in range(4):
        out[:, :, c * 128 : (c + 1) * 128] = obuf[c].astype(BF16)

    for a in range(3):
        wait_bytes(kbuf.at[pl.ds(0, 15 * BLOCK), :], s_qkv.at[a])

    @pl.when(jnp.logical_not(last))
    def _():
        wait_bytes(kbuf.at[pl.ds(0, 2 * WIN), :], s_halo.at[0])

    @pl.when(jnp.logical_not(first))
    def _():
        wait_bytes(kbuf.at[pl.ds(0, 2 * WIN), :], s_halo.at[1])

    wait_bytes(wq.at[pl.ds(0, 3 * PIECE), pl.ds(0, HALF)], s_w.at[0])
    wait_bytes(wq.at[pl.ds(0, 9 * PIECE), pl.ds(0, HALF)], s_w.at[1])
    wait_bytes(wq.at[pl.ds(0, 3 * SHARD), pl.ds(0, HALF)], s_w.at[2])
    wait_bytes(rbuf.at[pl.ds(0, 3)], s_res.at[0])
    wait_bytes(mbuf.at[pl.ds(0, 3)], s_res.at[1])
    wait_bytes(att.at[pl.ds(0, 3)], s_g.at[0])
    wait_bytes(gbuf.at[:, :, pl.ds(0, 3 * 512)], s_y.at[0])
    wait_bytes(msg.at[pl.ds(0, 3)], s_msg.at[0])
    for finish in finishes:
        finish()


def on_device(
    queries,
    head_keys,
    head_values,
    region_request,
    request_adapter,
    residual,
    output_gate,
    output_weight,
    adapter_down_factors,
    adapter_up_factors,
    closing_scale,
    closing_shift,
    patch_projection_weight,
    patch_projection_bias,
    convolution_kernel,
    convolution_bias,
):
    far = pl.BlockSpec(memory_space=pl.ANY)
    near = pl.BlockSpec(memory_space=pltpu.VMEM)
    scalars = pl.BlockSpec(memory_space=pltpu.SMEM)
    dma = pltpu.SemaphoreType.DMA
    return pl.pallas_call(
        kernel,
        out_shape=jax.ShapeDtypeStruct((16, 32, 512), BF16),
        in_specs=[
            far, far, far, near, scalars, far, near, far,
            near, far, near, near, near, near, near, near,
        ],
        out_specs=near,
        scratch_shapes=[
            pltpu.VMEM((BAND, HD), BF16),
            pltpu.VMEM((BAND + 2 * WIN, HD), BF16),
            pltpu.VMEM((BAND + 2 * WIN, HD), BF16),
            pltpu.VMEM((4, 4, BLOCK, HD), BF16),
            pltpu.VMEM((QUARTER, PAD_DEEP), BF16),
            pltpu.VMEM((128, QUARTER), BF16),
            pltpu.VMEM((4, BLOCK, QUARTER), BF16),
            pltpu.VMEM((4, BLOCK, RANKS), BF16),
            pltpu.VMEM((4, BLOCK, DEEP), BF16),
            pltpu.VMEM((BLOCK, QUARTER), F32),
            pltpu.VMEM((4, BLOCK + 8, 128), F32),
            pltpu.VMEM((4, BLOCK + 8, 128), F32),
            pltpu.VMEM((BLOCK, 128), BF16),
            pltpu.VMEM((10, 48, 128), BF16),
            pltpu.VMEM((10, 48, 128), F32),
            pltpu.VMEM((4, 512, 512), BF16),
            pltpu.VMEM((4, 16, 32, 128), F32),
            pltpu.VMEM((8, 128), F32),
            dma((3, 4)),
            dma((3,)),
            dma((2,)),
            dma((2,)),
            dma((2,)),
            dma((3,)),
            dma((3,)),
            dma((2,)),
            dma((2,)),
            dma((4,)),
            dma((1,)),
            dma((4,)),
            dma((1,)),
            dma((1,)),
            dma((1,)),
            dma((3,)),
            dma((27,)),
        ],
        compiler_params=pltpu.CompilerParams(
            collective_id=0, has_side_effects=True, vmem_limit_bytes=60 * 1024 * 1024
        ),
    )(
        queries,
        head_keys,
        head_values,
        region_request.reshape(1, -1),
        request_adapter,
        residual,
        output_gate.reshape(1, -1),
        output_weight.T,
        adapter_down_factors,
        adapter_up_factors.T,
        closing_scale.reshape(1, -1),
        closing_shift.reshape(1, -1),
        patch_projection_weight.T,
        patch_projection_bias.reshape(1, -1),
        convolution_kernel,
        convolution_bias.reshape(1, -1),
    )


def solution(mesh):
    return jax.shard_map(
        on_device,
        mesh=mesh,
        in_specs=(
            P(("seq", "tile"), None),
            P(("seq", "tile"), None),
            P(("seq", "tile"), None),
            P(("seq", "tile")),
            P(),
            P(("seq", "tile"), None),
            P(),
            P(None, "tile"),
            P(),
            P(None, "tile"),
            P(),
            P(),
            P(),
            P(),
            P(),
            P(),
        ),
        out_specs=P("seq", "tile", None),
        check_vma=False,
    )
```

```python
import math

import jax
import jax.numpy as jnp
from jax import lax
from jax.experimental import pallas as pl
from jax.experimental.pallas import tpu as pltpu
from jax.sharding import PartitionSpec as P

HD = 128
WIN = 512
SEQ = 32
TILE = 16
BLOCK = 128
BAND = 2048
FEATS = 2048
WIDTH = 3072
QUARTER = WIDTH // 4
SHARD = WIDTH // TILE
RANKS = 128
DEEP = FEATS + RANKS
PAD_DEEP = 2304
PIECE = SHARD // 4
HALF = PAD_DEEP // 2
KEYS = BLOCK + 2 * WIN

norm_epsilon = 1e-06
latent_scaling = 0.3611
latent_offset = 0.1159

MESH = pl.DeviceIdType.MESH
F32 = jnp.float32
BF16 = jnp.bfloat16


def wait_bytes(ref, sem):
    pltpu.make_async_copy(ref, ref, sem).wait()


def kernel(
    q_hbm,
    k_hbm,
    v_hbm,
    request,
    request_adapter,
    residual_hbm,
    gate,
    weight_hbm,
    down,
    up_hbm,
    scale,
    shift,
    patch_weight,
    patch_bias,
    conv_kernel,
    conv_bias,
    out,
    qbuf,
    kbuf,
    vbuf,
    att,
    wq,
    patch_wide,
    rbuf,
    mbuf,
    gbuf,
    xbuf,
    msg,
    msgin,
    lat,
    lbuf,
    lfull,
    wc,
    obuf,
    bias_row,
    r_qkv,
    s_qkv,
    r_halo,
    s_halo,
    l_w,
    r_w,
    s_w,
    r_res,
    s_res,
    r_g,
    s_g,
    r_y,
    s_y,
    r_msg,
    s_msg,
    r_lat,
    s_lat,
):
    t = lax.axis_index("tile")
    s = lax.axis_index("seq")
    y = t // 4
    z = lax.rem(t, 4)
    core = lax.rem(s, 2)
    x = s // 8
    sibling = s + 1 - 2 * core
    first = s == 0
    last = s == SEQ - 1

    def remote(src, dst, send_sem, recv_sem, where):
        return pltpu.make_async_remote_copy(
            src_ref=src,
            dst_ref=dst,
            send_sem=send_sem,
            recv_sem=recv_sem,
            device_id=where,
            device_id_type=MESH,
        )

    @pl.when(first)
    def _():
        kbuf[0:WIN, :] = jnp.zeros((WIN, HD), BF16)
        vbuf[0:WIN, :] = jnp.zeros((WIN, HD), BF16)
        lbuf[0] = jnp.zeros((48, 128), BF16)

    @pl.when(last)
    def _():
        kbuf[WIN + BAND :, :] = jnp.zeros((WIN, HD), BF16)
        vbuf[WIN + BAND :, :] = jnp.zeros((WIN, HD), BF16)
        lbuf[9] = jnp.zeros((48, 128), BF16)

    @pl.when(t == 0)
    def _():
        lbuf[:, 0:16, :] = jnp.zeros((10, 16, 128), BF16)

    @pl.when(t == TILE - 1)
    def _():
        lbuf[:, 32:48, :] = jnp.zeros((10, 16, 128), BF16)

    wq[:, DEEP:] = jnp.zeros((QUARTER, PAD_DEEP - DEEP), BF16)

    barrier = pltpu.get_barrier_semaphore()

    def greet(d, carry):
        pl.semaphore_signal(
            barrier, inc=1, device_id={"tile": lax.rem(t + d, TILE)}, device_id_type=MESH
        )
        return carry

    lax.fori_loop(1, TILE, greet, 0)
    for d in range(1, 4):
        pl.semaphore_signal(
            barrier, inc=1, device_id={"seq": lax.rem(s + 8 * d, SEQ)}, device_id_type=MESH
        )

    def ring(d):
        far = lax.rem(lax.rem(s // 2, 4) * 4 + z + d + 16, 16)
        return {"seq": (x * 4 + far // 4) * 2 + core, "tile": y * 4 + lax.rem(far, 4)}

    two = 2 - 4 * core
    for d in (1, -1, -two):
        pl.semaphore_signal(barrier, inc=1, device_id=ring(d), device_id_type=MESH)

    @pl.when(jnp.logical_not(first))
    def _():
        pl.semaphore_signal(barrier, inc=1, device_id={"seq": s - 1}, device_id_type=MESH)
        for p in (14, 15):
            pl.semaphore_signal(
                barrier, inc=1, device_id={"seq": s - 1, "tile": p}, device_id_type=MESH
            )

    @pl.when(jnp.logical_not(last))
    def _():
        pl.semaphore_signal(barrier, inc=1, device_id={"seq": s + 1}, device_id_type=MESH)
        for p in (0, 1):
            pl.semaphore_signal(
                barrier, inc=1, device_id={"seq": s + 1, "tile": p}, device_id_type=MESH
            )

    bottom = (t >= TILE - 2) & jnp.logical_not(last)
    top = (t <= 1) & jnp.logical_not(first)

    own_shard = pl.ds(pl.multiple_of(z * SHARD, 64), SHARD)
    w_local = pltpu.make_async_copy(weight_hbm, wq.at[own_shard, pl.ds(0, FEATS)], l_w.at[0])
    u_local = pltpu.make_async_copy(up_hbm, wq.at[own_shard, pl.ds(FEATS, RANKS)], l_w.at[1])
    w_local.start()
    u_local.start()

    pl.semaphore_wait(
        barrier,
        TILE
        + 5
        + jnp.where(first, 0, 1)
        + jnp.where(last, 0, 1)
        + jnp.where(bottom, TILE, 0)
        + jnp.where(top, TILE, 0),
    )

    half_cols = pl.ds(pl.multiple_of(core * HALF, 128), HALF)

    def piece(z2):
        return wq.at[pl.ds(pl.multiple_of(z2 * SHARD + x * PIECE, 16), PIECE), half_cols]


    own_rows = pl.ds(pl.multiple_of(WIN + t * BLOCK, BLOCK), BLOCK)
    own_q_rows = pl.ds(pl.multiple_of(t * BLOCK, BLOCK), BLOCK)
    sets = ((k_hbm, kbuf, own_rows), (v_hbm, vbuf, own_rows), (q_hbm, qbuf, own_q_rows))
    for a, (src, dst, rows) in enumerate(sets):
        if a == 2:
            w_local.wait()
            u_local.wait()
            for d in (1, -1, two):
                remote(piece(z), piece(z), s_w.at[0], r_w.at[0], ring(d)).start()

        def send(d, carry, a=a, src=src, dst=dst, rows=rows):
            p = lax.rem(t + d, TILE)
            cols = pl.ds(pl.multiple_of(p * HD, HD), HD)
            remote(
                src.at[:, cols], dst.at[rows, :], s_qkv.at[a], r_qkv.at[a, y], {"tile": p}
            ).start()
            return carry

        lax.fori_loop(1, TILE, send, 0)
        own_cols = pl.ds(pl.multiple_of(t * HD, HD), HD)
        pltpu.make_async_copy(src.at[:, own_cols], dst.at[rows, :], r_qkv.at[a, y]).start()

    adapters = jnp.zeros((1, BLOCK), jnp.int32)
    for r in range(8):
        adapters = adapters + jnp.where(request[...] == r, request_adapter[r], 0)
    owner = lax.broadcasted_iota(jnp.int32, (RANKS, BLOCK), 0) // 32
    kept = jnp.where(jnp.broadcast_to(adapters, (RANKS, BLOCK)) == owner, 1.0, 0.0)
    mbuf[y] = kept.T.astype(BF16)

    for d in range(4):
        y2 = lax.rem(y + d, 4)
        cols = pl.ds(pl.multiple_of(y2 * QUARTER, 128), QUARTER)
        if d == 0:
            pltpu.make_async_copy(residual_hbm.at[:, cols], rbuf.at[y], r_res.at[0]).start()
        else:
            where = {"tile": y2 * 4 + z}
            remote(
                residual_hbm.at[:, cols], rbuf.at[y], s_res.at[0], r_res.at[0], where
            ).start()
            remote(mbuf.at[y], mbuf.at[y], s_res.at[1], r_res.at[1], where).start()

    wait_bytes(wq.at[pl.ds(0, 3 * PIECE), pl.ds(0, HALF)], r_w.at[0])
    for d in range(1, 4):
        ref = piece(lax.rem(z + d, 4))
        for e in range(1, 4):
            remote(
                ref, ref, s_w.at[1], r_w.at[1], {"seq": lax.rem(s + 8 * e, SEQ)}
            ).start()

    flat_kernel = conv_kernel[...].reshape(144, 512)
    place = lax.broadcasted_iota(jnp.int32, (512, 144), 0)
    tap = lax.broadcasted_iota(jnp.int32, (512, 144), 1)
    lane = lax.rem(place, 128)
    dri = place // 256
    dwi = lax.rem(place // 128, 2)
    pa = lax.rem(lane // 2, 2)
    pb = lax.rem(lane, 2)
    for a in range(2):
        for b in range(2):
            ky = 2 * dri + a + pa - 1
            kx = 2 * dwi + b + pb - 1
            good = (
                (lane < 64)
                & (ky >= 0)
                & (ky < 3)
                & (kx >= 0)
                & (kx < 3)
                & (tap == (ky * 3 + kx) * 16 + lane // 4)
            )
            pick = jnp.where(good, 1.0, 0.0).astype(BF16)
            wc[2 * a + b] = jnp.dot(pick, flat_kernel, preferred_element_type=F32).astype(BF16)
    bias_row[...] = jnp.zeros((8, 128), F32)
    bias_row[0:1, 0:64] = patch_bias[...]

    quarter = pl.ds(pl.multiple_of(y * QUARTER, 128), QUARTER)
    patch_wide[0:64, :] = patch_weight[:, quarter]
    patch_wide[64:128, :] = jnp.zeros((64, QUARTER), BF16)
    across = (((1,), (1,)), ((), ()))
    gain = 1.0 + scale[:, quarter]
    which = lax.broadcasted_iota(jnp.int32, (8, QUARTER), 0)
    pair = jnp.where(which == 0, gain, jnp.where(which == 1, shift[:, quarter], 0.0))
    sums = lax.dot_general(
        pair,
        patch_wide[...].astype(F32),
        across,
        precision=lax.Precision.HIGHEST,
        preferred_element_type=F32,
    )

    for row in (3, 0):
        for a in range(2):
            buf = (kbuf, vbuf)[a]
            wait_bytes(buf.at[pl.ds(WIN, 4 * BLOCK), :], r_qkv.at[a, row])

    def halo(buf, a, up):
        if up:
            src = buf.at[pl.ds(WIN + 3 * WIN, WIN), :]
            dst = buf.at[pl.ds(0, WIN), :]
            return remote(src, dst, s_halo.at[0], r_halo.at[0], {"seq": s + 1})
        src = buf.at[pl.ds(WIN, WIN), :]
        dst = buf.at[pl.ds(WIN + BAND, WIN), :]
        return remote(src, dst, s_halo.at[1], r_halo.at[1], {"seq": s - 1})

    def send_halo(row):
        @pl.when((row == 3) & jnp.logical_not(last))
        def _():
            halo(kbuf, 0, True).start()
            halo(vbuf, 1, True).start()

        @pl.when((row == 0) & jnp.logical_not(first))
        def _():
            halo(kbuf, 0, False).start()
            halo(vbuf, 1, False).start()

    row_a = jnp.where(core == 0, 3, 0)
    row_b = 3 - row_a
    send_halo(row_a)

    for row in (1, 2):
        for a in range(2):
            buf = (kbuf, vbuf)[a]
            wait_bytes(buf.at[pl.ds(WIN, 4 * BLOCK), :], r_qkv.at[a, row])
    for row in range(4):
        wait_bytes(qbuf.at[pl.ds(0, 4 * BLOCK), :], r_qkv.at[2, row])

    factor = math.log2(math.e) / math.sqrt(HD)
    row_at = lax.broadcasted_iota(jnp.int32, (BLOCK, BLOCK), 0)
    col_at = lax.broadcasted_iota(jnp.int32, (BLOCK, BLOCK), 1)

    head_cols = pl.ds(pl.multiple_of(t * HD, HD), HD)

    def send_heads(row, b):
        @pl.when(z == b)
        def _():
            dst = gbuf.at[row, :, head_cols]
            pltpu.make_async_copy(att.at[row, b], dst, r_g.at[row, z]).start()
            for d in range(1, 4):
                where = {"tile": lax.rem(y + d, 4) * 4 + z}
                remote(att.at[row, b], dst, s_y.at[0], r_y.at[row], where).start()

        @pl.when(z != b)
        def _():
            remote(
                att.at[row, b],
                gbuf.at[row, :, head_cols],
                s_g.at[0],
                r_g.at[row, z],
                {"tile": y * 4 + b},
            ).start()

    def send_group(row):
        order = (
            jnp.where(z < 3, z + 1, 2),
            jnp.where(z == 0, 2, jnp.where(z == 3, 1, z - 1)),
            jnp.where(z < 2, 3, 0),
        )
        for z2 in order:
            ref = gbuf.at[row, :, pl.ds(pl.multiple_of((y * 4 + z2) * HD, HD), HD)]
            wait_bytes(gbuf.at[row, :, pl.ds(0, HD)], r_g.at[row, z2])
            for d in range(1, 4):
                where = {"tile": lax.rem(y + d, 4) * 4 + z}
                remote(ref, ref, s_y.at[0], r_y.at[row], where).start()
        wait_bytes(gbuf.at[row, :, pl.ds(0, HD)], r_g.at[row, z])

    def attend(row):
        edge = (first & (row == 0)) | (last & (row == 3))

        def block(b, edged):
            start = pl.multiple_of(row * WIN + b * BLOCK, BLOCK)
            q = qbuf[pl.ds(start, BLOCK), :]
            k = kbuf[pl.ds(start, KEYS), :]
            v = vbuf[pl.ds(start, KEYS), :]
            scores = lax.dot_general(
                q, k, (((1,), (1,)), ((), ())), preferred_element_type=F32
            )
            low = jnp.where(col_at >= row_at, scores[:, :BLOCK], -jnp.inf)
            high = jnp.where(col_at <= row_at, scores[:, KEYS - BLOCK :], -jnp.inf)
            scores = jnp.concatenate([low, scores[:, BLOCK : KEYS - BLOCK], high], axis=1)
            if edged:
                key_at = start + lax.broadcasted_iota(jnp.int32, (BLOCK, KEYS), 1)
                least = jnp.where(first, WIN, 0)
                most = jnp.where(last, WIN + BAND, 2 * WIN + BAND)
                scores = jnp.where((key_at >= least) & (key_at < most), scores, -jnp.inf)
            highest = jnp.max(scores, axis=1, keepdims=True)
            expons = jnp.exp2((scores - highest) * factor)
            totals = jnp.sum(expons, axis=1, keepdims=True)
            weighted = jnp.dot(expons.astype(BF16), v, preferred_element_type=F32)
            att[row, b] = (weighted / totals).astype(BF16)
            send_heads(row, b)

        @pl.when(edge)
        def _():
            for b in range(4):
                block(b, True)

        @pl.when(jnp.logical_not(edge))
        def _():
            for b in range(4):
                block(b, False)

    def wait_halo(row):
        missing = (first & (row == 0)) | (last & (row == 3))

        @pl.when(jnp.logical_not(missing))
        def _():
            wait_bytes(kbuf.at[pl.ds(0, 2 * WIN), :], r_halo.at[jnp.where(row == 0, 0, 1)])

    def project(row):
        wait_bytes(gbuf.at[row, :, pl.ds(0, 3 * 512)], r_y.at[row])
        lowered = jnp.dot(gbuf[row, :, pl.ds(0, FEATS)], down[...], preferred_element_type=F32)
        lowered = jnp.where(mbuf[row] > 0, lowered, 0.0).astype(BF16)
        gbuf[row, :, pl.ds(FEATS, RANKS)] = lowered
        total = jnp.zeros((BLOCK, 1), F32)
        for n in range(3):
            cols = pl.ds(n * 256, 256)
            gate_cols = pl.ds(pl.multiple_of(y * QUARTER + n * 256, 128), 256)
            branch = lax.dot_general(
                gbuf[row],
                wq[pl.ds(n * 256, 256), pl.ds(0, DEEP)],
                across,
                preferred_element_type=F32,
            )
            base = rbuf[row, :, cols].astype(F32)
            value = (base + gate[:, gate_cols] * branch).astype(BF16).astype(F32)
            xbuf[:, cols] = value
            total = total + jnp.sum(value, axis=1, keepdims=True)
        average = total * (1.0 / QUARTER)
        centered = xbuf[...] - average
        squares = jnp.sum(centered * centered, axis=1, keepdims=True)
        part = lax.dot_general(
            (centered * gain).astype(BF16), patch_wide[...], across, preferred_element_type=F32
        )
        lane_at = lax.broadcasted_iota(jnp.int32, (BLOCK, 128), 1)
        part = jnp.where(lane_at == 64, average, jnp.where(lane_at == 65, squares, part))
        msg[row, 0:BLOCK, :] = part
        msg[row, BLOCK : BLOCK + 8, :] = sums

        @pl.when(row == y)
        def _():
            pltpu.make_async_copy(msg.at[row], msgin.at[y], r_msg.at[0]).start()

        @pl.when(row != y)
        def _():
            where = {"tile": row * 4 + z}
            remote(msg.at[row], msgin.at[y], s_msg.at[0], r_msg.at[0], where).start()

    half = lax.rem(t, 2)
    line = t // 2 + 1

    def hand(i, target, src, dst, shift, sending):
        recv = r_lat.at[y if shift == 0 else 4 if shift == 1 else 5]
        if shift == 0:
            far = remote(src, dst, s_lat.at[i], recv, {"tile": target})
            away = target != t
        else:
            where = {"seq": s + shift, "tile": target}
            far = remote(src, dst, s_lat.at[i], recv, where)
            away = sending

        def begin():
            if shift == 0:

                @pl.when(target == t)
                def _():
                    pltpu.make_async_copy(src, dst, recv).start()

            @pl.when(away)
            def _():
                far.start()

        def finish():
            @pl.when(away)
            def _():
                far.wait_send()

        return begin, finish

    hands = []
    cross_src = pl.ds(pl.multiple_of(112 * (1 - half), 16), 16)
    cross_dst = pl.ds(pl.multiple_of(32 * half, 16), 16)
    for k, (shift, sending, at) in enumerate(((1, bottom, 0), (-1, top, 9), (0, None, line))):
        for i in range(8):
            begin = max(0, i - 1) * 16
            size = min(8, i + 2) * 16 - begin
            src = lat.at[pl.ds(begin, size), :]
            dst = lbuf.at[at, pl.ds(16 if i == 0 else 0, size), :]
            hands.append(hand(9 * k + i, half * 8 + i, src, dst, shift, sending))
        src = lat.at[cross_src, :]
        dst = lbuf.at[at, cross_dst, :]
        hands.append(hand(9 * k + 8, 8 - half, src, dst, shift, sending))
    def finish_home():
        wait_bytes(msgin, r_msg.at[0])

        means = [msgin[i, 0:BLOCK, 64:65] for i in range(4)]
        spreads = [msgin[i, 0:BLOCK, 65:66] for i in range(4)]
        overall = (means[0] + means[1] + means[2] + means[3]) * 0.25
        variance = spreads[0] + spreads[1] + spreads[2] + spreads[3]
        projected = jnp.zeros((BLOCK, 128), F32)
        constant = bias_row[0:1, :]
        for i in range(4):
            off = means[i] - overall
            variance = variance + QUARTER * off * off
            projected = projected + (
                msgin[i, 0:BLOCK, :] + off * msgin[i, BLOCK : BLOCK + 1, :]
            )
            constant = constant + msgin[i, BLOCK + 1 : BLOCK + 2, :]
        projected = projected * lax.rsqrt(variance * (1.0 / WIDTH) + norm_epsilon) + constant
        latents = projected / latent_scaling + latent_offset
        small = lax.broadcasted_iota(jnp.int32, (BLOCK, 128), 1) < 64
        lat[...] = jnp.where(small, latents, 0.0).astype(BF16)

        for begin, _ in hands:
            begin()

    attend(1)
    attend(2)
    wait_halo(row_a)
    attend(row_a)
    send_halo(row_b)
    wait_bytes(wq.at[pl.ds(0, 9 * PIECE), pl.ds(0, HALF)], r_w.at[1])
    for d in range(1, 4):
        z2 = lax.rem(z + d, 4)
        ref = wq.at[pl.ds(pl.multiple_of(z2 * SHARD, 64), SHARD), half_cols]
        remote(ref, ref, s_w.at[2], r_w.at[2], {"seq": sibling}).start()
    send_group(1)
    send_group(2)
    wait_bytes(wq.at[pl.ds(0, 3 * SHARD), pl.ds(0, HALF)], r_w.at[2])
    wait_bytes(rbuf, r_res.at[0])
    wait_bytes(mbuf.at[pl.ds(0, 3)], r_res.at[1])
    project(1)
    send_group(row_a)
    wait_halo(row_b)
    attend(row_b)
    project(2)
    send_group(row_b)
    project(row_a)

    @pl.when(y != row_b)
    def _():
        finish_home()

    project(row_b)

    @pl.when(y == row_b)
    def _():
        finish_home()

    side = (t == 0) | (t == TILE - 1)

    def wait_lines(begin, count, sem):
        @pl.when(side)
        def _():
            wait_bytes(lbuf.at[pl.ds(begin, count), pl.ds(0, 32), :], sem)

        @pl.when(jnp.logical_not(side))
        def _():
            wait_bytes(lbuf.at[pl.ds(begin, count), :, :], sem)

    def convolve(begin, count):
        lines = pl.ds(begin, count + 2)
        lfull[lines] = lbuf[lines].astype(F32)
        columns = [lfull[lines, 15 + i : 31 + i, :].astype(BF16) for i in range(3)]
        for a in range(2):
            for b in range(2):
                near = jnp.concatenate(
                    [
                        columns[j + b][i + a : i + a + count].reshape(16 * count, 128)
                        for i in range(2)
                        for j in range(2)
                    ],
                    axis=1,
                )
                value = (
                    jnp.dot(near, wc[2 * a + b], preferred_element_type=F32) + conv_bias[...]
                ).reshape(count, 16, 512)
                for r in range(count):
                    for c in range(4):
                        obuf[c, 2 * (begin + r) + a, pl.ds(b, 16, stride=2), :] = value[
                            r, :, c * 128 : (c + 1) * 128
                        ]
        rows = pl.ds(2 * begin, 2 * count)
        for c in range(4):
            out[rows, :, c * 128 : (c + 1) * 128] = obuf[c, rows].astype(BF16)

    for row in (1, 2, row_a):
        wait_lines(2 * row + 1, 2, r_lat.at[row])

    @pl.when((core == 0) & jnp.logical_not(last))
    def _():
        wait_lines(9, 1, r_lat.at[5])

    @pl.when((core == 1) & jnp.logical_not(first))
    def _():
        wait_lines(0, 1, r_lat.at[4])

    convolve(jnp.where(core == 0, 3, 0), 5)
    wait_lines(2 * row_b + 1, 2, r_lat.at[row_b])

    @pl.when((core == 0) & jnp.logical_not(first))
    def _():
        wait_lines(0, 1, r_lat.at[4])

    @pl.when((core == 1) & jnp.logical_not(last))
    def _():
        wait_lines(9, 1, r_lat.at[5])

    convolve(jnp.where(core == 0, 0, 5), 3)

    for a in range(3):
        wait_bytes(kbuf.at[pl.ds(0, 15 * BLOCK), :], s_qkv.at[a])

    @pl.when(jnp.logical_not(last))
    def _():
        wait_bytes(kbuf.at[pl.ds(0, 2 * WIN), :], s_halo.at[0])

    @pl.when(jnp.logical_not(first))
    def _():
        wait_bytes(kbuf.at[pl.ds(0, 2 * WIN), :], s_halo.at[1])

    wait_bytes(wq.at[pl.ds(0, 3 * PIECE), pl.ds(0, HALF)], s_w.at[0])
    wait_bytes(wq.at[pl.ds(0, 9 * PIECE), pl.ds(0, HALF)], s_w.at[1])
    wait_bytes(wq.at[pl.ds(0, 3 * SHARD), pl.ds(0, HALF)], s_w.at[2])
    wait_bytes(rbuf.at[pl.ds(0, 3)], s_res.at[0])
    wait_bytes(mbuf.at[pl.ds(0, 3)], s_res.at[1])
    wait_bytes(att.at[pl.ds(0, 3)], s_g.at[0])
    wait_bytes(gbuf.at[:, :, pl.ds(0, 3 * 512)], s_y.at[0])
    wait_bytes(msg.at[pl.ds(0, 3)], s_msg.at[0])
    for _, finish in hands:
        finish()


def on_device(
    queries,
    head_keys,
    head_values,
    region_request,
    request_adapter,
    residual,
    output_gate,
    output_weight,
    adapter_down_factors,
    adapter_up_factors,
    closing_scale,
    closing_shift,
    patch_projection_weight,
    patch_projection_bias,
    convolution_kernel,
    convolution_bias,
):
    far = pl.BlockSpec(memory_space=pl.ANY)
    near = pl.BlockSpec(memory_space=pltpu.VMEM)
    scalars = pl.BlockSpec(memory_space=pltpu.SMEM)
    dma = pltpu.SemaphoreType.DMA
    return pl.pallas_call(
        kernel,
        out_shape=jax.ShapeDtypeStruct((16, 32, 512), BF16),
        in_specs=[
            far, far, far, near, scalars, far, near, far,
            near, far, near, near, near, near, near, near,
        ],
        out_specs=near,
        scratch_shapes=[
            pltpu.VMEM((BAND, HD), BF16),
            pltpu.VMEM((BAND + 2 * WIN, HD), BF16),
            pltpu.VMEM((BAND + 2 * WIN, HD), BF16),
            pltpu.VMEM((4, 4, BLOCK, HD), BF16),
            pltpu.VMEM((QUARTER, PAD_DEEP), BF16),
            pltpu.VMEM((128, QUARTER), BF16),
            pltpu.VMEM((4, BLOCK, QUARTER), BF16),
            pltpu.VMEM((4, BLOCK, RANKS), BF16),
            pltpu.VMEM((4, BLOCK, DEEP), BF16),
            pltpu.VMEM((BLOCK, QUARTER), F32),
            pltpu.VMEM((4, BLOCK + 8, 128), F32),
            pltpu.VMEM((4, BLOCK + 8, 128), F32),
            pltpu.VMEM((BLOCK, 128), BF16),
            pltpu.VMEM((10, 48, 128), BF16),
            pltpu.VMEM((10, 48, 128), F32),
            pltpu.VMEM((4, 512, 512), BF16),
            pltpu.VMEM((4, 16, 32, 128), F32),
            pltpu.VMEM((8, 128), F32),
            dma((3, 4)),
            dma((3,)),
            dma((2,)),
            dma((2,)),
            dma((2,)),
            dma((3,)),
            dma((3,)),
            dma((2,)),
            dma((2,)),
            dma((4, 4)),
            dma((1,)),
            dma((4,)),
            dma((1,)),
            dma((1,)),
            dma((1,)),
            dma((6,)),
            dma((27,)),
        ],
        compiler_params=pltpu.CompilerParams(
            collective_id=0, has_side_effects=True, vmem_limit_bytes=60 * 1024 * 1024
        ),
    )(
        queries,
        head_keys,
        head_values,
        region_request.reshape(1, -1),
        request_adapter,
        residual,
        output_gate.reshape(1, -1),
        output_weight.T,
        adapter_down_factors,
        adapter_up_factors.T,
        closing_scale.reshape(1, -1),
        closing_shift.reshape(1, -1),
        patch_projection_weight.T,
        patch_projection_bias.reshape(1, -1),
        convolution_kernel,
        convolution_bias.reshape(1, -1),
    )


def solution(mesh):
    return jax.shard_map(
        on_device,
        mesh=mesh,
        in_specs=(
            P(("seq", "tile"), None),
            P(("seq", "tile"), None),
            P(("seq", "tile"), None),
            P(("seq", "tile")),
            P(),
            P(("seq", "tile"), None),
            P(),
            P(None, "tile"),
            P(),
            P(None, "tile"),
            P(),
            P(),
            P(),
            P(),
            P(),
            P(),
        ),
        out_specs=P("seq", "tile", None),
        check_vma=False,
    )
```

```python
import math

import jax
import jax.numpy as jnp
from jax import lax
from jax.experimental import pallas as pl
from jax.experimental.pallas import tpu as pltpu
from jax.sharding import PartitionSpec as P

HD = 128
WIN = 512
SEQ = 32
TILE = 16
BLOCK = 128
BAND = 2048
FEATS = 2048
WIDTH = 3072
QUARTER = WIDTH // 4
SHARD = WIDTH // TILE
RANKS = 128
DEEP = FEATS + RANKS
PAD_DEEP = 2304
PIECE = SHARD // 4
HALF = PAD_DEEP // 2
KEYS = BLOCK + 2 * WIN

norm_epsilon = 1e-06
latent_scaling = 0.3611
latent_offset = 0.1159

MESH = pl.DeviceIdType.MESH
F32 = jnp.float32
BF16 = jnp.bfloat16


def wait_bytes(ref, sem):
    pltpu.make_async_copy(ref, ref, sem).wait()


def kernel(
    q_hbm,
    k_hbm,
    v_hbm,
    request,
    request_adapter,
    residual_hbm,
    gate,
    weight_hbm,
    down,
    up_hbm,
    scale,
    shift,
    patch_weight,
    patch_bias,
    conv_kernel,
    conv_bias,
    out,
    qbuf,
    kbuf,
    vbuf,
    att,
    wq,
    patch_wide,
    rbuf,
    mbuf,
    gbuf,
    xbuf,
    msg,
    msgin,
    lat,
    lbuf,
    lfull,
    wc,
    obuf,
    bias_row,
    r_qkv,
    s_qkv,
    r_halo,
    s_halo,
    l_w,
    r_w,
    s_w,
    r_res,
    s_res,
    r_g,
    s_g,
    r_y,
    s_y,
    r_msg,
    s_msg,
    r_lat,
    s_lat,
):
    t = lax.axis_index("tile")
    s = lax.axis_index("seq")
    y = t // 4
    z = lax.rem(t, 4)
    core = lax.rem(s, 2)
    x = s // 8
    sibling = s + 1 - 2 * core
    first = s == 0
    last = s == SEQ - 1

    def remote(src, dst, send_sem, recv_sem, where):
        return pltpu.make_async_remote_copy(
            src_ref=src,
            dst_ref=dst,
            send_sem=send_sem,
            recv_sem=recv_sem,
            device_id=where,
            device_id_type=MESH,
        )

    @pl.when(first)
    def _():
        kbuf[0:WIN, :] = jnp.zeros((WIN, HD), BF16)
        vbuf[0:WIN, :] = jnp.zeros((WIN, HD), BF16)
        lbuf[0] = jnp.zeros((48, 128), BF16)

    @pl.when(last)
    def _():
        kbuf[WIN + BAND :, :] = jnp.zeros((WIN, HD), BF16)
        vbuf[WIN + BAND :, :] = jnp.zeros((WIN, HD), BF16)
        lbuf[9] = jnp.zeros((48, 128), BF16)

    @pl.when(t == 0)
    def _():
        lbuf[:, 0:16, :] = jnp.zeros((10, 16, 128), BF16)

    @pl.when(t == TILE - 1)
    def _():
        lbuf[:, 32:48, :] = jnp.zeros((10, 16, 128), BF16)

    wq[:, DEEP:] = jnp.zeros((QUARTER, PAD_DEEP - DEEP), BF16)

    barrier = pltpu.get_barrier_semaphore()

    def greet(d, carry):
        pl.semaphore_signal(
            barrier, inc=1, device_id={"tile": lax.rem(t + d, TILE)}, device_id_type=MESH
        )
        return carry

    lax.fori_loop(1, TILE, greet, 0)
    for d in range(1, 4):
        pl.semaphore_signal(
            barrier, inc=1, device_id={"seq": lax.rem(s + 8 * d, SEQ)}, device_id_type=MESH
        )

    def ring(d):
        far = lax.rem(lax.rem(s // 2, 4) * 4 + z + d + 16, 16)
        return {"seq": (x * 4 + far // 4) * 2 + core, "tile": y * 4 + lax.rem(far, 4)}

    two = 2 - 4 * core
    for d in (1, -1, -two):
        pl.semaphore_signal(barrier, inc=1, device_id=ring(d), device_id_type=MESH)

    @pl.when(jnp.logical_not(first))
    def _():
        pl.semaphore_signal(barrier, inc=1, device_id={"seq": s - 1}, device_id_type=MESH)
        for p in (14, 15):
            pl.semaphore_signal(
                barrier, inc=1, device_id={"seq": s - 1, "tile": p}, device_id_type=MESH
            )

    @pl.when(jnp.logical_not(last))
    def _():
        pl.semaphore_signal(barrier, inc=1, device_id={"seq": s + 1}, device_id_type=MESH)
        for p in (0, 1):
            pl.semaphore_signal(
                barrier, inc=1, device_id={"seq": s + 1, "tile": p}, device_id_type=MESH
            )

    bottom = (t >= TILE - 2) & jnp.logical_not(last)
    top = (t <= 1) & jnp.logical_not(first)

    own_shard = pl.ds(pl.multiple_of(z * SHARD, 64), SHARD)
    w_local = pltpu.make_async_copy(weight_hbm, wq.at[own_shard, pl.ds(0, FEATS)], l_w.at[0])
    u_local = pltpu.make_async_copy(up_hbm, wq.at[own_shard, pl.ds(FEATS, RANKS)], l_w.at[1])
    w_local.start()
    u_local.start()

    pl.semaphore_wait(
        barrier,
        TILE
        + 5
        + jnp.where(first, 0, 1)
        + jnp.where(last, 0, 1)
        + jnp.where(bottom, TILE, 0)
        + jnp.where(top, TILE, 0),
    )

    half_cols = pl.ds(pl.multiple_of(core * HALF, 128), HALF)

    def piece(z2):
        return wq.at[pl.ds(pl.multiple_of(z2 * SHARD + x * PIECE, 16), PIECE), half_cols]


    own_rows = pl.ds(pl.multiple_of(WIN + t * BLOCK, BLOCK), BLOCK)
    own_q_rows = pl.ds(pl.multiple_of(t * BLOCK, BLOCK), BLOCK)
    sets = ((k_hbm, kbuf, own_rows), (v_hbm, vbuf, own_rows), (q_hbm, qbuf, own_q_rows))
    for a, (src, dst, rows) in enumerate(sets):

        def send(d, carry, a=a, src=src, dst=dst, rows=rows):
            p = lax.rem(t + d, TILE)
            cols = pl.ds(pl.multiple_of(p * HD, HD), HD)
            remote(
                src.at[:, cols], dst.at[rows, :], s_qkv.at[a], r_qkv.at[a, y], {"tile": p}
            ).start()
            return carry

        lax.fori_loop(1, TILE, send, 0)
        own_cols = pl.ds(pl.multiple_of(t * HD, HD), HD)
        pltpu.make_async_copy(src.at[:, own_cols], dst.at[rows, :], r_qkv.at[a, y]).start()

    adapters = jnp.zeros((1, BLOCK), jnp.int32)
    for r in range(8):
        adapters = adapters + jnp.where(request[...] == r, request_adapter[r], 0)
    owner = lax.broadcasted_iota(jnp.int32, (RANKS, BLOCK), 0) // 32
    kept = jnp.where(jnp.broadcast_to(adapters, (RANKS, BLOCK)) == owner, 1.0, 0.0)
    mbuf[y] = kept.T.astype(BF16)

    for d in range(4):
        y2 = lax.rem(y + d, 4)
        cols = pl.ds(pl.multiple_of(y2 * QUARTER, 128), QUARTER)
        if d == 0:
            pltpu.make_async_copy(residual_hbm.at[:, cols], rbuf.at[y], r_res.at[0]).start()
        else:
            where = {"tile": y2 * 4 + z}
            remote(
                residual_hbm.at[:, cols], rbuf.at[y], s_res.at[0], r_res.at[0], where
            ).start()
            remote(mbuf.at[y], mbuf.at[y], s_res.at[1], r_res.at[1], where).start()

    w_local.wait()
    u_local.wait()
    for d in (1, -1, two):
        remote(piece(z), piece(z), s_w.at[0], r_w.at[0], ring(d)).start()

    flat_kernel = conv_kernel[...].reshape(144, 512)
    place = lax.broadcasted_iota(jnp.int32, (512, 144), 0)
    tap = lax.broadcasted_iota(jnp.int32, (512, 144), 1)
    lane = lax.rem(place, 128)
    dri = place // 256
    dwi = lax.rem(place // 128, 2)
    pa = lax.rem(lane // 2, 2)
    pb = lax.rem(lane, 2)
    for a in range(2):
        for b in range(2):
            ky = 2 * dri + a + pa - 1
            kx = 2 * dwi + b + pb - 1
            good = (
                (lane < 64)
                & (ky >= 0)
                & (ky < 3)
                & (kx >= 0)
                & (kx < 3)
                & (tap == (ky * 3 + kx) * 16 + lane // 4)
            )
            pick = jnp.where(good, 1.0, 0.0).astype(BF16)
            wc[2 * a + b] = jnp.dot(pick, flat_kernel, preferred_element_type=F32).astype(BF16)
    bias_row[...] = jnp.zeros((8, 128), F32)
    bias_row[0:1, 0:64] = patch_bias[...]

    quarter = pl.ds(pl.multiple_of(y * QUARTER, 128), QUARTER)
    patch_wide[0:64, :] = patch_weight[:, quarter]
    patch_wide[64:128, :] = jnp.zeros((64, QUARTER), BF16)
    across = (((1,), (1,)), ((), ()))
    gain = 1.0 + scale[:, quarter]
    which = lax.broadcasted_iota(jnp.int32, (8, QUARTER), 0)
    pair = jnp.where(which == 0, gain, jnp.where(which == 1, shift[:, quarter], 0.0))
    sums = lax.dot_general(
        pair,
        patch_wide[...].astype(F32),
        across,
        precision=lax.Precision.HIGHEST,
        preferred_element_type=F32,
    )

    for row in (3, 0):
        for a in range(2):
            buf = (kbuf, vbuf)[a]
            wait_bytes(buf.at[pl.ds(WIN, 4 * BLOCK), :], r_qkv.at[a, row])

    def halo(buf, a, up):
        if up:
            src = buf.at[pl.ds(WIN + 3 * WIN, WIN), :]
            dst = buf.at[pl.ds(0, WIN), :]
            return remote(src, dst, s_halo.at[0], r_halo.at[0], {"seq": s + 1})
        src = buf.at[pl.ds(WIN, WIN), :]
        dst = buf.at[pl.ds(WIN + BAND, WIN), :]
        return remote(src, dst, s_halo.at[1], r_halo.at[1], {"seq": s - 1})

    def send_halo(row):
        @pl.when((row == 3) & jnp.logical_not(last))
        def _():
            halo(kbuf, 0, True).start()
            halo(vbuf, 1, True).start()

        @pl.when((row == 0) & jnp.logical_not(first))
        def _():
            halo(kbuf, 0, False).start()
            halo(vbuf, 1, False).start()

    row_a = jnp.where(core == 0, 3, 0)
    row_b = 3 - row_a
    send_halo(row_a)

    for row in (1, 2):
        for a in range(2):
            buf = (kbuf, vbuf)[a]
            wait_bytes(buf.at[pl.ds(WIN, 4 * BLOCK), :], r_qkv.at[a, row])
    for row in range(4):
        wait_bytes(qbuf.at[pl.ds(0, 4 * BLOCK), :], r_qkv.at[2, row])

    factor = math.log2(math.e) / math.sqrt(HD)
    row_at = lax.broadcasted_iota(jnp.int32, (BLOCK, BLOCK), 0)
    col_at = lax.broadcasted_iota(jnp.int32, (BLOCK, BLOCK), 1)

    head_cols = pl.ds(pl.multiple_of(t * HD, HD), HD)

    def send_heads(row, b):
        @pl.when(z == b)
        def _():
            dst = gbuf.at[row, :, head_cols]
            pltpu.make_async_copy(att.at[row, b], dst, r_g.at[row, z]).start()
            for d in range(1, 4):
                where = {"tile": lax.rem(y + d, 4) * 4 + z}
                remote(att.at[row, b], dst, s_y.at[0], r_y.at[row], where).start()

        @pl.when(z != b)
        def _():
            remote(
                att.at[row, b],
                gbuf.at[row, :, head_cols],
                s_g.at[0],
                r_g.at[row, z],
                {"tile": y * 4 + b},
            ).start()

    def send_group(row):
        order = (
            jnp.where(z < 3, z + 1, 2),
            jnp.where(z == 0, 2, jnp.where(z == 3, 1, z - 1)),
            jnp.where(z < 2, 3, 0),
        )
        for z2 in order:
            ref = gbuf.at[row, :, pl.ds(pl.multiple_of((y * 4 + z2) * HD, HD), HD)]
            wait_bytes(gbuf.at[row, :, pl.ds(0, HD)], r_g.at[row, z2])
            for d in range(1, 4):
                where = {"tile": lax.rem(y + d, 4) * 4 + z}
                remote(ref, ref, s_y.at[0], r_y.at[row], where).start()
        wait_bytes(gbuf.at[row, :, pl.ds(0, HD)], r_g.at[row, z])

    def attend(row):
        edge = (first & (row == 0)) | (last & (row == 3))

        def block(b, edged):
            start = pl.multiple_of(row * WIN + b * BLOCK, BLOCK)
            q = qbuf[pl.ds(start, BLOCK), :]
            k = kbuf[pl.ds(start, KEYS), :]
            v = vbuf[pl.ds(start, KEYS), :]
            scores = lax.dot_general(
                q, k, (((1,), (1,)), ((), ())), preferred_element_type=F32
            )
            low = jnp.where(col_at >= row_at, scores[:, :BLOCK], -jnp.inf)
            high = jnp.where(col_at <= row_at, scores[:, KEYS - BLOCK :], -jnp.inf)
            scores = jnp.concatenate([low, scores[:, BLOCK : KEYS - BLOCK], high], axis=1)
            if edged:
                key_at = start + lax.broadcasted_iota(jnp.int32, (BLOCK, KEYS), 1)
                least = jnp.where(first, WIN, 0)
                most = jnp.where(last, WIN + BAND, 2 * WIN + BAND)
                scores = jnp.where((key_at >= least) & (key_at < most), scores, -jnp.inf)
            highest = jnp.max(scores, axis=1, keepdims=True)
            expons = jnp.exp2((scores - highest) * factor)
            totals = jnp.sum(expons, axis=1, keepdims=True)
            weighted = jnp.dot(expons.astype(BF16), v, preferred_element_type=F32)
            att[row, b] = (weighted / totals).astype(BF16)
            send_heads(row, b)

        @pl.when(edge)
        def _():
            for b in range(4):
                block(b, True)

        @pl.when(jnp.logical_not(edge))
        def _():
            for b in range(4):
                block(b, False)

    def wait_halo(row):
        missing = (first & (row == 0)) | (last & (row == 3))

        @pl.when(jnp.logical_not(missing))
        def _():
            wait_bytes(kbuf.at[pl.ds(0, 2 * WIN), :], r_halo.at[jnp.where(row == 0, 0, 1)])

    def project(row):
        wait_bytes(gbuf.at[row, :, pl.ds(0, 3 * 512)], r_y.at[row])
        lowered = jnp.dot(gbuf[row, :, pl.ds(0, FEATS)], down[...], preferred_element_type=F32)
        lowered = jnp.where(mbuf[row] > 0, lowered, 0.0).astype(BF16)
        gbuf[row, :, pl.ds(FEATS, RANKS)] = lowered
        total = jnp.zeros((BLOCK, 1), F32)
        for n in range(3):
            cols = pl.ds(n * 256, 256)
            gate_cols = pl.ds(pl.multiple_of(y * QUARTER + n * 256, 128), 256)
            branch = lax.dot_general(
                gbuf[row],
                wq[pl.ds(n * 256, 256), pl.ds(0, DEEP)],
                across,
                preferred_element_type=F32,
            )
            base = rbuf[row, :, cols].astype(F32)
            value = (base + gate[:, gate_cols] * branch).astype(BF16).astype(F32)
            xbuf[:, cols] = value
            total = total + jnp.sum(value, axis=1, keepdims=True)
        average = total * (1.0 / QUARTER)
        centered = xbuf[...] - average
        squares = jnp.sum(centered * centered, axis=1, keepdims=True)
        part = lax.dot_general(
            (centered * gain).astype(BF16), patch_wide[...], across, preferred_element_type=F32
        )
        lane_at = lax.broadcasted_iota(jnp.int32, (BLOCK, 128), 1)
        stats = jnp.where(lane_at == 0, average, jnp.where(lane_at == 1, squares, 0.0))
        msg[row, 0:64, :] = part[0:64] + pltpu.roll(part[64:BLOCK], 64, axis=1)
        msg[row, 64:72, :] = stats.T[0:8]
        msg[row, 72:80, :] = sums

        @pl.when(row == y)
        def _():
            pltpu.make_async_copy(msg.at[row], msgin.at[y], r_msg.at[0]).start()

        @pl.when(row != y)
        def _():
            where = {"tile": row * 4 + z}
            remote(msg.at[row], msgin.at[y], s_msg.at[0], r_msg.at[0], where).start()

    half = lax.rem(t, 2)
    line = t // 2 + 1

    def hand(i, target, src, dst, shift, sending):
        recv = r_lat.at[y if shift == 0 else 4 if shift == 1 else 5]
        if shift == 0:
            far = remote(src, dst, s_lat.at[i], recv, {"tile": target})
            away = target != t
        else:
            where = {"seq": s + shift, "tile": target}
            far = remote(src, dst, s_lat.at[i], recv, where)
            away = sending

        def begin():
            if shift == 0:

                @pl.when(target == t)
                def _():
                    pltpu.make_async_copy(src, dst, recv).start()

            @pl.when(away)
            def _():
                far.start()

        def finish():
            @pl.when(away)
            def _():
                far.wait_send()

        return begin, finish

    hands = []
    cross_src = pl.ds(pl.multiple_of(112 * (1 - half), 16), 16)
    cross_dst = pl.ds(pl.multiple_of(32 * half, 16), 16)
    for k, (shift, sending, at) in enumerate(((1, bottom, 0), (-1, top, 9), (0, None, line))):
        for i in range(8):
            begin = max(0, i - 1) * 16
            size = min(8, i + 2) * 16 - begin
            src = lat.at[pl.ds(begin, size), :]
            dst = lbuf.at[at, pl.ds(16 if i == 0 else 0, size), :]
            hands.append(hand(9 * k + i, half * 8 + i, src, dst, shift, sending))
        src = lat.at[cross_src, :]
        dst = lbuf.at[at, cross_dst, :]
        hands.append(hand(9 * k + 8, 8 - half, src, dst, shift, sending))
    def finish_home():
        wait_bytes(msgin, r_msg.at[0])

        packed = msgin[0, 0:64, :] + msgin[1, 0:64, :] + msgin[2, 0:64, :] + msgin[3, 0:64, :]
        projected = jnp.concatenate([packed, pltpu.roll(packed, 64, axis=1)], axis=0)
        stats = jnp.concatenate(
            [msgin[i, 64:72, :] for i in range(4)] + [jnp.zeros((96, 128), F32)], axis=0
        ).T
        means = [stats[:, 8 * i : 8 * i + 1] for i in range(4)]
        spreads = [stats[:, 8 * i + 1 : 8 * i + 2] for i in range(4)]
        overall = (means[0] + means[1] + means[2] + means[3]) * 0.25
        variance = spreads[0] + spreads[1] + spreads[2] + spreads[3]
        constant = bias_row[0:1, :]
        for i in range(4):
            off = means[i] - overall
            variance = variance + QUARTER * off * off
            projected = projected + off * msgin[i, 72:73, :]
            constant = constant + msgin[i, 73:74, :]
        projected = projected * lax.rsqrt(variance * (1.0 / WIDTH) + norm_epsilon) + constant
        latents = projected / latent_scaling + latent_offset
        small = lax.broadcasted_iota(jnp.int32, (BLOCK, 128), 1) < 64
        lat[...] = jnp.where(small, latents, 0.0).astype(BF16)

        for begin, _ in hands:
            begin()

    attend(1)
    attend(2)
    wait_bytes(wq.at[pl.ds(0, 3 * PIECE), pl.ds(0, HALF)], r_w.at[0])
    for d in range(1, 4):
        ref = piece(lax.rem(z + d, 4))
        for e in range(1, 4):
            remote(
                ref, ref, s_w.at[1], r_w.at[1], {"seq": lax.rem(s + 8 * e, SEQ)}
            ).start()
    wait_halo(row_a)
    attend(row_a)
    send_halo(row_b)
    send_group(1)
    send_group(2)
    send_group(row_a)
    wait_bytes(wq.at[pl.ds(0, 9 * PIECE), pl.ds(0, HALF)], r_w.at[1])
    for d in range(1, 4):
        z2 = lax.rem(z + d, 4)
        ref = wq.at[pl.ds(pl.multiple_of(z2 * SHARD, 64), SHARD), half_cols]
        remote(ref, ref, s_w.at[2], r_w.at[2], {"seq": sibling}).start()
    wait_halo(row_b)
    attend(row_b)
    wait_bytes(wq.at[pl.ds(0, 3 * SHARD), pl.ds(0, HALF)], r_w.at[2])
    wait_bytes(rbuf, r_res.at[0])
    wait_bytes(mbuf.at[pl.ds(0, 3)], r_res.at[1])
    project(1)
    send_group(row_b)
    project(2)
    project(row_a)

    inner = (y == 1) | (y == 2)

    @pl.when(inner)
    def _():
        finish_home()

    project(row_b)

    @pl.when(jnp.logical_not(inner))
    def _():
        finish_home()

    side = (t == 0) | (t == TILE - 1)

    def wait_lines(begin, count, sem):
        @pl.when(side)
        def _():
            wait_bytes(lbuf.at[pl.ds(begin, count), pl.ds(0, 32), :], sem)

        @pl.when(jnp.logical_not(side))
        def _():
            wait_bytes(lbuf.at[pl.ds(begin, count), :, :], sem)

    def convolve(begin, count):
        lines = pl.ds(begin, count + 2)
        lfull[lines] = lbuf[lines].astype(F32)
        columns = [lfull[lines, 15 + i : 31 + i, :].astype(BF16) for i in range(3)]
        for a in range(2):
            for b in range(2):
                near = jnp.concatenate(
                    [
                        columns[j + b][i + a : i + a + count].reshape(16 * count, 128)
                        for i in range(2)
                        for j in range(2)
                    ],
                    axis=1,
                )
                value = (
                    jnp.dot(near, wc[2 * a + b], preferred_element_type=F32) + conv_bias[...]
                ).reshape(count, 16, 512)
                for r in range(count):
                    for c in range(4):
                        obuf[c, 2 * (begin + r) + a, pl.ds(b, 16, stride=2), :] = value[
                            r, :, c * 128 : (c + 1) * 128
                        ]
        rows = pl.ds(2 * begin, 2 * count)
        for c in range(4):
            out[rows, :, c * 128 : (c + 1) * 128] = obuf[c, rows].astype(BF16)

    for row in (1, 2, row_a):
        wait_lines(2 * row + 1, 2, r_lat.at[row])

    @pl.when((core == 0) & jnp.logical_not(last))
    def _():
        wait_lines(9, 1, r_lat.at[5])

    @pl.when((core == 1) & jnp.logical_not(first))
    def _():
        wait_lines(0, 1, r_lat.at[4])

    convolve(jnp.where(core == 0, 3, 0), 5)
    wait_lines(2 * row_b + 1, 2, r_lat.at[row_b])

    @pl.when((core == 0) & jnp.logical_not(first))
    def _():
        wait_lines(0, 1, r_lat.at[4])

    @pl.when((core == 1) & jnp.logical_not(last))
    def _():
        wait_lines(9, 1, r_lat.at[5])

    convolve(jnp.where(core == 0, 0, 5), 3)

    for a in range(3):
        wait_bytes(kbuf.at[pl.ds(0, 15 * BLOCK), :], s_qkv.at[a])

    @pl.when(jnp.logical_not(last))
    def _():
        wait_bytes(kbuf.at[pl.ds(0, 2 * WIN), :], s_halo.at[0])

    @pl.when(jnp.logical_not(first))
    def _():
        wait_bytes(kbuf.at[pl.ds(0, 2 * WIN), :], s_halo.at[1])

    wait_bytes(wq.at[pl.ds(0, 3 * PIECE), pl.ds(0, HALF)], s_w.at[0])
    wait_bytes(wq.at[pl.ds(0, 9 * PIECE), pl.ds(0, HALF)], s_w.at[1])
    wait_bytes(wq.at[pl.ds(0, 3 * SHARD), pl.ds(0, HALF)], s_w.at[2])
    wait_bytes(rbuf.at[pl.ds(0, 3)], s_res.at[0])
    wait_bytes(mbuf.at[pl.ds(0, 3)], s_res.at[1])
    wait_bytes(att.at[pl.ds(0, 3)], s_g.at[0])
    wait_bytes(gbuf.at[:, :, pl.ds(0, 3 * 512)], s_y.at[0])
    wait_bytes(msg.at[pl.ds(0, 3)], s_msg.at[0])
    for _, finish in hands:
        finish()


def on_device(
    queries,
    head_keys,
    head_values,
    region_request,
    request_adapter,
    residual,
    output_gate,
    output_weight,
    adapter_down_factors,
    adapter_up_factors,
    closing_scale,
    closing_shift,
    patch_projection_weight,
    patch_projection_bias,
    convolution_kernel,
    convolution_bias,
):
    far = pl.BlockSpec(memory_space=pl.ANY)
    near = pl.BlockSpec(memory_space=pltpu.VMEM)
    scalars = pl.BlockSpec(memory_space=pltpu.SMEM)
    dma = pltpu.SemaphoreType.DMA
    return pl.pallas_call(
        kernel,
        out_shape=jax.ShapeDtypeStruct((16, 32, 512), BF16),
        in_specs=[
            far, far, far, near, scalars, far, near, far,
            near, far, near, near, near, near, near, near,
        ],
        out_specs=near,
        scratch_shapes=[
            pltpu.VMEM((BAND, HD), BF16),
            pltpu.VMEM((BAND + 2 * WIN, HD), BF16),
            pltpu.VMEM((BAND + 2 * WIN, HD), BF16),
            pltpu.VMEM((4, 4, BLOCK, HD), BF16),
            pltpu.VMEM((QUARTER, PAD_DEEP), BF16),
            pltpu.VMEM((128, QUARTER), BF16),
            pltpu.VMEM((4, BLOCK, QUARTER), BF16),
            pltpu.VMEM((4, BLOCK, RANKS), BF16),
            pltpu.VMEM((4, BLOCK, DEEP), BF16),
            pltpu.VMEM((BLOCK, QUARTER), F32),
            pltpu.VMEM((4, 80, 128), F32),
            pltpu.VMEM((4, 80, 128), F32),
            pltpu.VMEM((BLOCK, 128), BF16),
            pltpu.VMEM((10, 48, 128), BF16),
            pltpu.VMEM((10, 48, 128), F32),
            pltpu.VMEM((4, 512, 512), BF16),
            pltpu.VMEM((4, 16, 32, 128), F32),
            pltpu.VMEM((8, 128), F32),
            dma((3, 4)),
            dma((3,)),
            dma((2,)),
            dma((2,)),
            dma((2,)),
            dma((3,)),
            dma((3,)),
            dma((2,)),
            dma((2,)),
            dma((4, 4)),
            dma((1,)),
            dma((4,)),
            dma((1,)),
            dma((1,)),
            dma((1,)),
            dma((6,)),
            dma((27,)),
        ],
        compiler_params=pltpu.CompilerParams(
            collective_id=0, has_side_effects=True, vmem_limit_bytes=60 * 1024 * 1024
        ),
    )(
        queries,
        head_keys,
        head_values,
        region_request.reshape(1, -1),
        request_adapter,
        residual,
        output_gate.reshape(1, -1),
        output_weight.T,
        adapter_down_factors,
        adapter_up_factors.T,
        closing_scale.reshape(1, -1),
        closing_shift.reshape(1, -1),
        patch_projection_weight.T,
        patch_projection_bias.reshape(1, -1),
        convolution_kernel,
        convolution_bias.reshape(1, -1),
    )


def solution(mesh):
    return jax.shard_map(
        on_device,
        mesh=mesh,
        in_specs=(
            P(("seq", "tile"), None),
            P(("seq", "tile"), None),
            P(("seq", "tile"), None),
            P(("seq", "tile")),
            P(),
            P(("seq", "tile"), None),
            P(),
            P(None, "tile"),
            P(),
            P(None, "tile"),
            P(),
            P(),
            P(),
            P(),
            P(),
            P(),
        ),
        out_specs=P("seq", "tile", None),
        check_vma=False,
    )
```

```python
import math

import jax
import jax.numpy as jnp
from jax import lax
from jax.experimental import pallas as pl
from jax.experimental.pallas import tpu as pltpu
from jax.sharding import PartitionSpec as P

HD = 128
WIN = 512
SEQ = 32
TILE = 16
BLOCK = 128
BAND = 2048
FEATS = 2048
WIDTH = 3072
QUARTER = WIDTH // 4
SHARD = WIDTH // TILE
RANKS = 128
DEEP = FEATS + RANKS
PAD_DEEP = 2304
PIECE = SHARD // 4
HALF = PAD_DEEP // 2
KEYS = BLOCK + 2 * WIN

norm_epsilon = 1e-06
latent_scaling = 0.3611
latent_offset = 0.1159

MESH = pl.DeviceIdType.MESH
F32 = jnp.float32
BF16 = jnp.bfloat16


def wait_bytes(ref, sem):
    pltpu.make_async_copy(ref, ref, sem).wait()


def kernel(
    q_hbm,
    k_hbm,
    v_hbm,
    request,
    request_adapter,
    residual_hbm,
    gate,
    weight_hbm,
    down,
    up_hbm,
    scale,
    shift,
    patch_weight,
    patch_bias,
    conv_kernel,
    conv_bias,
    out,
    qbuf,
    kbuf,
    vbuf,
    att,
    wq,
    patch_wide,
    rbuf,
    mbuf,
    gbuf,
    xbuf,
    msg,
    msgin,
    lat,
    lbuf,
    lfull,
    wc,
    obuf,
    bias_row,
    r_qkv,
    s_qkv,
    r_halo,
    s_halo,
    l_w,
    r_w,
    s_w,
    r_res,
    s_res,
    r_g,
    s_g,
    r_y,
    s_y,
    r_msg,
    s_msg,
    r_lat,
    s_lat,
):
    t = lax.axis_index("tile")
    s = lax.axis_index("seq")
    y = t // 4
    z = lax.rem(t, 4)
    core = lax.rem(s, 2)
    x = s // 8
    sibling = s + 1 - 2 * core
    first = s == 0
    last = s == SEQ - 1

    def remote(src, dst, send_sem, recv_sem, where):
        return pltpu.make_async_remote_copy(
            src_ref=src,
            dst_ref=dst,
            send_sem=send_sem,
            recv_sem=recv_sem,
            device_id=where,
            device_id_type=MESH,
        )

    @pl.when(first)
    def _():
        kbuf[0:WIN, :] = jnp.zeros((WIN, HD), BF16)
        vbuf[0:WIN, :] = jnp.zeros((WIN, HD), BF16)
        lbuf[0] = jnp.zeros((48, 128), BF16)

    @pl.when(last)
    def _():
        kbuf[WIN + BAND :, :] = jnp.zeros((WIN, HD), BF16)
        vbuf[WIN + BAND :, :] = jnp.zeros((WIN, HD), BF16)
        lbuf[9] = jnp.zeros((48, 128), BF16)

    @pl.when(t == 0)
    def _():
        lbuf[:, 0:16, :] = jnp.zeros((10, 16, 128), BF16)

    @pl.when(t == TILE - 1)
    def _():
        lbuf[:, 32:48, :] = jnp.zeros((10, 16, 128), BF16)

    wq[:, DEEP:] = jnp.zeros((QUARTER, PAD_DEEP - DEEP), BF16)

    barrier = pltpu.get_barrier_semaphore()

    def greet(d, carry):
        pl.semaphore_signal(
            barrier, inc=1, device_id={"tile": lax.rem(t + d, TILE)}, device_id_type=MESH
        )
        return carry

    lax.fori_loop(1, TILE, greet, 0)
    for d in range(1, 4):
        pl.semaphore_signal(
            barrier, inc=1, device_id={"seq": lax.rem(s + 8 * d, SEQ)}, device_id_type=MESH
        )

    def ring(d):
        far = lax.rem(lax.rem(s // 2, 4) * 4 + z + d + 16, 16)
        return {"seq": (x * 4 + far // 4) * 2 + core, "tile": y * 4 + lax.rem(far, 4)}

    two = 2 - 4 * core
    for d in (1, -1, -two):
        pl.semaphore_signal(barrier, inc=1, device_id=ring(d), device_id_type=MESH)

    @pl.when(jnp.logical_not(first))
    def _():
        pl.semaphore_signal(barrier, inc=1, device_id={"seq": s - 1}, device_id_type=MESH)
        for p in (14, 15):
            pl.semaphore_signal(
                barrier, inc=1, device_id={"seq": s - 1, "tile": p}, device_id_type=MESH
            )

    @pl.when(jnp.logical_not(last))
    def _():
        pl.semaphore_signal(barrier, inc=1, device_id={"seq": s + 1}, device_id_type=MESH)
        for p in (0, 1):
            pl.semaphore_signal(
                barrier, inc=1, device_id={"seq": s + 1, "tile": p}, device_id_type=MESH
            )

    bottom = (t >= TILE - 2) & jnp.logical_not(last)
    top = (t <= 1) & jnp.logical_not(first)

    own_shard = pl.ds(pl.multiple_of(z * SHARD, 64), SHARD)
    w_local = pltpu.make_async_copy(weight_hbm, wq.at[own_shard, pl.ds(0, FEATS)], l_w.at[0])
    u_local = pltpu.make_async_copy(up_hbm, wq.at[own_shard, pl.ds(FEATS, RANKS)], l_w.at[1])
    w_local.start()
    u_local.start()

    pl.semaphore_wait(
        barrier,
        TILE
        + 5
        + jnp.where(first, 0, 1)
        + jnp.where(last, 0, 1)
        + jnp.where(bottom, TILE, 0)
        + jnp.where(top, TILE, 0),
    )

    half_cols = pl.ds(pl.multiple_of(core * HALF, 128), HALF)

    def piece(z2):
        return wq.at[pl.ds(pl.multiple_of(z2 * SHARD + x * PIECE, 16), PIECE), half_cols]


    own_rows = pl.ds(pl.multiple_of(WIN + t * BLOCK, BLOCK), BLOCK)
    own_q_rows = pl.ds(pl.multiple_of(t * BLOCK, BLOCK), BLOCK)
    sets = ((k_hbm, kbuf, own_rows), (v_hbm, vbuf, own_rows), (q_hbm, qbuf, own_q_rows))
    for a, (src, dst, rows) in enumerate(sets):

        def send(d, carry, a=a, src=src, dst=dst, rows=rows):
            p = lax.rem(t + d, TILE)
            cols = pl.ds(pl.multiple_of(p * HD, HD), HD)
            remote(
                src.at[:, cols], dst.at[rows, :], s_qkv.at[a], r_qkv.at[a, y], {"tile": p}
            ).start()
            return carry

        lax.fori_loop(1, TILE, send, 0)
        own_cols = pl.ds(pl.multiple_of(t * HD, HD), HD)
        pltpu.make_async_copy(src.at[:, own_cols], dst.at[rows, :], r_qkv.at[a, y]).start()

    w_local.wait()
    u_local.wait()
    for d in (1, -1, two):
        remote(piece(z), piece(z), s_w.at[0], r_w.at[0], ring(d)).start()

    adapters = jnp.zeros((1, BLOCK), jnp.int32)
    for r in range(8):
        adapters = adapters + jnp.where(request[...] == r, request_adapter[r], 0)
    owner = lax.broadcasted_iota(jnp.int32, (RANKS, BLOCK), 0) // 32
    kept = jnp.where(jnp.broadcast_to(adapters, (RANKS, BLOCK)) == owner, 1.0, 0.0)
    mbuf[y] = kept.T.astype(BF16)

    for d in range(4):
        y2 = lax.rem(y + d, 4)
        cols = pl.ds(pl.multiple_of(y2 * QUARTER, 128), QUARTER)
        if d == 0:
            pltpu.make_async_copy(residual_hbm.at[:, cols], rbuf.at[y], r_res.at[0]).start()
        else:
            where = {"tile": y2 * 4 + z}
            remote(
                residual_hbm.at[:, cols], rbuf.at[y], s_res.at[0], r_res.at[0], where
            ).start()
            remote(mbuf.at[y], mbuf.at[y], s_res.at[1], r_res.at[1], where).start()


    flat_kernel = conv_kernel[...].reshape(144, 512)
    place = lax.broadcasted_iota(jnp.int32, (512, 144), 0)
    tap = lax.broadcasted_iota(jnp.int32, (512, 144), 1)
    lane = lax.rem(place, 128)
    dri = place // 256
    dwi = lax.rem(place // 128, 2)
    pa = lax.rem(lane // 2, 2)
    pb = lax.rem(lane, 2)
    for a in range(2):
        for b in range(2):
            ky = 2 * dri + a + pa - 1
            kx = 2 * dwi + b + pb - 1
            good = (
                (lane < 64)
                & (ky >= 0)
                & (ky < 3)
                & (kx >= 0)
                & (kx < 3)
                & (tap == (ky * 3 + kx) * 16 + lane // 4)
            )
            pick = jnp.where(good, 1.0, 0.0).astype(BF16)
            wc[2 * a + b] = jnp.dot(pick, flat_kernel, preferred_element_type=F32).astype(BF16)
    bias_row[...] = jnp.zeros((8, 128), F32)
    bias_row[0:1, 0:64] = patch_bias[...]

    quarter = pl.ds(pl.multiple_of(y * QUARTER, 128), QUARTER)
    patch_wide[0:64, :] = patch_weight[:, quarter]
    patch_wide[64:128, :] = jnp.zeros((64, QUARTER), BF16)
    across = (((1,), (1,)), ((), ()))
    gain = 1.0 + scale[:, quarter]
    which = lax.broadcasted_iota(jnp.int32, (8, QUARTER), 0)
    pair = jnp.where(which == 0, gain, jnp.where(which == 1, shift[:, quarter], 0.0))
    sums = lax.dot_general(
        pair,
        patch_wide[...].astype(F32),
        across,
        precision=lax.Precision.HIGHEST,
        preferred_element_type=F32,
    )

    for row in (3, 0):
        for a in range(2):
            buf = (kbuf, vbuf)[a]
            wait_bytes(buf.at[pl.ds(WIN, 4 * BLOCK), :], r_qkv.at[a, row])

    def halo(buf, a, up):
        if up:
            src = buf.at[pl.ds(WIN + 3 * WIN, WIN), :]
            dst = buf.at[pl.ds(0, WIN), :]
            return remote(src, dst, s_halo.at[0], r_halo.at[0], {"seq": s + 1})
        src = buf.at[pl.ds(WIN, WIN), :]
        dst = buf.at[pl.ds(WIN + BAND, WIN), :]
        return remote(src, dst, s_halo.at[1], r_halo.at[1], {"seq": s - 1})

    def send_halo(row):
        @pl.when((row == 3) & jnp.logical_not(last))
        def _():
            halo(kbuf, 0, True).start()
            halo(vbuf, 1, True).start()

        @pl.when((row == 0) & jnp.logical_not(first))
        def _():
            halo(kbuf, 0, False).start()
            halo(vbuf, 1, False).start()

    row_a = jnp.where(core == 0, 3, 0)
    row_b = 3 - row_a
    send_halo(row_a)

    for row in (1, 2):
        for a in range(2):
            buf = (kbuf, vbuf)[a]
            wait_bytes(buf.at[pl.ds(WIN, 4 * BLOCK), :], r_qkv.at[a, row])
    for row in range(4):
        wait_bytes(qbuf.at[pl.ds(0, 4 * BLOCK), :], r_qkv.at[2, row])

    factor = math.log2(math.e) / math.sqrt(HD)
    row_at = lax.broadcasted_iota(jnp.int32, (BLOCK, BLOCK), 0)
    col_at = lax.broadcasted_iota(jnp.int32, (BLOCK, BLOCK), 1)

    head_cols = pl.ds(pl.multiple_of(t * HD, HD), HD)

    def send_heads(row, b):
        @pl.when(z == b)
        def _():
            dst = gbuf.at[row, :, head_cols]
            pltpu.make_async_copy(att.at[row, b], dst, r_g.at[row, z]).start()
            for d in range(1, 4):
                where = {"tile": lax.rem(y + d, 4) * 4 + z}
                remote(att.at[row, b], dst, s_y.at[0], r_y.at[row], where).start()

        @pl.when(z != b)
        def _():
            remote(
                att.at[row, b],
                gbuf.at[row, :, head_cols],
                s_g.at[0],
                r_g.at[row, z],
                {"tile": y * 4 + b},
            ).start()

    def send_group(row):
        order = (
            jnp.where(z < 3, z + 1, 2),
            jnp.where(z == 0, 2, jnp.where(z == 3, 1, z - 1)),
            jnp.where(z < 2, 3, 0),
        )
        for z2 in order:
            ref = gbuf.at[row, :, pl.ds(pl.multiple_of((y * 4 + z2) * HD, HD), HD)]
            wait_bytes(gbuf.at[row, :, pl.ds(0, HD)], r_g.at[row, z2])
            for d in range(1, 4):
                where = {"tile": lax.rem(y + d, 4) * 4 + z}
                remote(ref, ref, s_y.at[0], r_y.at[row], where).start()
        wait_bytes(gbuf.at[row, :, pl.ds(0, HD)], r_g.at[row, z])

    def attend(row):
        edge = (first & (row == 0)) | (last & (row == 3))

        def block(b, edged):
            start = pl.multiple_of(row * WIN + b * BLOCK, BLOCK)
            q = qbuf[pl.ds(start, BLOCK), :]
            k = kbuf[pl.ds(start, KEYS), :]
            v = vbuf[pl.ds(start, KEYS), :]
            scores = lax.dot_general(
                q, k, (((1,), (1,)), ((), ())), preferred_element_type=F32
            )
            low = jnp.where(col_at >= row_at, scores[:, :BLOCK], -jnp.inf)
            high = jnp.where(col_at <= row_at, scores[:, KEYS - BLOCK :], -jnp.inf)
            scores = jnp.concatenate([low, scores[:, BLOCK : KEYS - BLOCK], high], axis=1)
            if edged:
                key_at = start + lax.broadcasted_iota(jnp.int32, (BLOCK, KEYS), 1)
                least = jnp.where(first, WIN, 0)
                most = jnp.where(last, WIN + BAND, 2 * WIN + BAND)
                scores = jnp.where((key_at >= least) & (key_at < most), scores, -jnp.inf)
            highest = jnp.max(scores, axis=1, keepdims=True)
            expons = jnp.exp2((scores - highest) * factor)
            totals = jnp.sum(expons, axis=1, keepdims=True)
            weighted = jnp.dot(expons.astype(BF16), v, preferred_element_type=F32)
            att[row, b] = (weighted / totals).astype(BF16)
            send_heads(row, b)

        @pl.when(edge)
        def _():
            for b in range(4):
                block(b, True)

        @pl.when(jnp.logical_not(edge))
        def _():
            for b in range(4):
                block(b, False)

    def wait_halo(row):
        missing = (first & (row == 0)) | (last & (row == 3))

        @pl.when(jnp.logical_not(missing))
        def _():
            wait_bytes(kbuf.at[pl.ds(0, 2 * WIN), :], r_halo.at[jnp.where(row == 0, 0, 1)])

    def project(row):
        wait_bytes(gbuf.at[row, :, pl.ds(0, 3 * 512)], r_y.at[row])
        lowered = jnp.dot(gbuf[row, :, pl.ds(0, FEATS)], down[...], preferred_element_type=F32)
        lowered = jnp.where(mbuf[row] > 0, lowered, 0.0).astype(BF16)
        gbuf[row, :, pl.ds(FEATS, RANKS)] = lowered
        total = jnp.zeros((BLOCK, 1), F32)
        for n in range(3):
            cols = pl.ds(n * 256, 256)
            gate_cols = pl.ds(pl.multiple_of(y * QUARTER + n * 256, 128), 256)
            branch = lax.dot_general(
                gbuf[row],
                wq[pl.ds(n * 256, 256), pl.ds(0, DEEP)],
                across,
                preferred_element_type=F32,
            )
            base = rbuf[row, :, cols].astype(F32)
            value = (base + gate[:, gate_cols] * branch).astype(BF16).astype(F32)
            xbuf[:, cols] = value
            total = total + jnp.sum(value, axis=1, keepdims=True)
        average = total * (1.0 / QUARTER)
        centered = xbuf[...] - average
        squares = jnp.sum(centered * centered, axis=1, keepdims=True)
        part = lax.dot_general(
            (centered * gain).astype(BF16), patch_wide[...], across, preferred_element_type=F32
        )
        lane_at = lax.broadcasted_iota(jnp.int32, (BLOCK, 128), 1)
        stats = jnp.where(lane_at == 0, average, jnp.where(lane_at == 1, squares, 0.0))
        msg[row, 0:64, :] = part[0:64] + pltpu.roll(part[64:BLOCK], 64, axis=1)
        msg[row, 64:72, :] = stats.T[0:8]
        msg[row, 72:80, :] = sums

        @pl.when(row == y)
        def _():
            pltpu.make_async_copy(msg.at[row], msgin.at[y], r_msg.at[0]).start()

        @pl.when(row != y)
        def _():
            where = {"tile": row * 4 + z}
            remote(msg.at[row], msgin.at[y], s_msg.at[0], r_msg.at[0], where).start()

    half = lax.rem(t, 2)
    line = t // 2 + 1

    def hand(i, target, src, dst, shift, sending):
        recv = r_lat.at[y if shift == 0 else 4 if shift == 1 else 5]
        if shift == 0:
            far = remote(src, dst, s_lat.at[i], recv, {"tile": target})
            away = target != t
        else:
            where = {"seq": s + shift, "tile": target}
            far = remote(src, dst, s_lat.at[i], recv, where)
            away = sending

        def begin():
            if shift == 0:

                @pl.when(target == t)
                def _():
                    pltpu.make_async_copy(src, dst, recv).start()

            @pl.when(away)
            def _():
                far.start()

        def finish():
            @pl.when(away)
            def _():
                far.wait_send()

        return begin, finish

    hands = []
    cross_src = pl.ds(pl.multiple_of(112 * (1 - half), 16), 16)
    cross_dst = pl.ds(pl.multiple_of(32 * half, 16), 16)
    for k, (shift, sending, at) in enumerate(((1, bottom, 0), (-1, top, 9), (0, None, line))):
        for i in range(8):
            begin = max(0, i - 1) * 16
            size = min(8, i + 2) * 16 - begin
            src = lat.at[pl.ds(begin, size), :]
            dst = lbuf.at[at, pl.ds(16 if i == 0 else 0, size), :]
            hands.append(hand(9 * k + i, half * 8 + i, src, dst, shift, sending))
        src = lat.at[cross_src, :]
        dst = lbuf.at[at, cross_dst, :]
        hands.append(hand(9 * k + 8, 8 - half, src, dst, shift, sending))
    def finish_home():
        wait_bytes(msgin, r_msg.at[0])

        packed = msgin[0, 0:64, :] + msgin[1, 0:64, :] + msgin[2, 0:64, :] + msgin[3, 0:64, :]
        projected = jnp.concatenate([packed, pltpu.roll(packed, 64, axis=1)], axis=0)
        stats = jnp.concatenate(
            [msgin[i, 64:72, :] for i in range(4)] + [jnp.zeros((96, 128), F32)], axis=0
        ).T
        means = [stats[:, 8 * i : 8 * i + 1] for i in range(4)]
        spreads = [stats[:, 8 * i + 1 : 8 * i + 2] for i in range(4)]
        overall = (means[0] + means[1] + means[2] + means[3]) * 0.25
        variance = spreads[0] + spreads[1] + spreads[2] + spreads[3]
        constant = bias_row[0:1, :]
        for i in range(4):
            off = means[i] - overall
            variance = variance + QUARTER * off * off
            projected = projected + off * msgin[i, 72:73, :]
            constant = constant + msgin[i, 73:74, :]
        projected = projected * lax.rsqrt(variance * (1.0 / WIDTH) + norm_epsilon) + constant
        latents = projected / latent_scaling + latent_offset
        small = lax.broadcasted_iota(jnp.int32, (BLOCK, 128), 1) < 64
        lat[...] = jnp.where(small, latents, 0.0).astype(BF16)

        for begin, _ in hands:
            begin()

    attend(1)
    attend(2)
    wait_bytes(wq.at[pl.ds(0, 3 * PIECE), pl.ds(0, HALF)], r_w.at[0])
    for d in range(1, 4):
        ref = piece(lax.rem(z + d, 4))
        for e in range(1, 4):
            remote(
                ref, ref, s_w.at[1], r_w.at[1], {"seq": lax.rem(s + 8 * e, SEQ)}
            ).start()
    wait_halo(row_a)
    attend(row_a)
    send_halo(row_b)
    send_group(1)
    send_group(2)
    send_group(row_a)
    wait_bytes(wq.at[pl.ds(0, 9 * PIECE), pl.ds(0, HALF)], r_w.at[1])
    for d in range(1, 4):
        z2 = lax.rem(z + d, 4)
        ref = wq.at[pl.ds(pl.multiple_of(z2 * SHARD, 64), SHARD), half_cols]
        remote(ref, ref, s_w.at[2], r_w.at[2], {"seq": sibling}).start()
    wait_halo(row_b)
    attend(row_b)
    wait_bytes(wq.at[pl.ds(0, 3 * SHARD), pl.ds(0, HALF)], r_w.at[2])
    wait_bytes(rbuf, r_res.at[0])
    wait_bytes(mbuf.at[pl.ds(0, 3)], r_res.at[1])
    project(1)
    send_group(row_b)
    project(2)
    project(row_a)

    inner = (y == 1) | (y == 2)

    @pl.when(inner)
    def _():
        finish_home()

    project(row_b)

    @pl.when(jnp.logical_not(inner))
    def _():
        finish_home()

    side = (t == 0) | (t == TILE - 1)

    def wait_lines(begin, count, sem):
        @pl.when(side)
        def _():
            wait_bytes(lbuf.at[pl.ds(begin, count), pl.ds(0, 32), :], sem)

        @pl.when(jnp.logical_not(side))
        def _():
            wait_bytes(lbuf.at[pl.ds(begin, count), :, :], sem)

    def convolve(begin, count):
        lines = pl.ds(begin, count + 2)
        lfull[lines] = lbuf[lines].astype(F32)
        columns = [lfull[lines, 15 + i : 31 + i, :].astype(BF16) for i in range(3)]
        for a in range(2):
            for b in range(2):
                near = jnp.concatenate(
                    [
                        columns[j + b][i + a : i + a + count].reshape(16 * count, 128)
                        for i in range(2)
                        for j in range(2)
                    ],
                    axis=1,
                )
                value = (
                    jnp.dot(near, wc[2 * a + b], preferred_element_type=F32) + conv_bias[...]
                ).reshape(count, 16, 512)
                for r in range(count):
                    for c in range(4):
                        obuf[c, 2 * (begin + r) + a, pl.ds(b, 16, stride=2), :] = value[
                            r, :, c * 128 : (c + 1) * 128
                        ]
        rows = pl.ds(2 * begin, 2 * count)
        for c in range(4):
            out[rows, :, c * 128 : (c + 1) * 128] = obuf[c, rows].astype(BF16)

    for row in (1, 2, row_a):
        wait_lines(2 * row + 1, 2, r_lat.at[row])

    @pl.when((core == 0) & jnp.logical_not(last))
    def _():
        wait_lines(9, 1, r_lat.at[5])

    @pl.when((core == 1) & jnp.logical_not(first))
    def _():
        wait_lines(0, 1, r_lat.at[4])

    convolve(jnp.where(core == 0, 3, 0), 5)
    wait_lines(2 * row_b + 1, 2, r_lat.at[row_b])

    @pl.when((core == 0) & jnp.logical_not(first))
    def _():
        wait_lines(0, 1, r_lat.at[4])

    @pl.when((core == 1) & jnp.logical_not(last))
    def _():
        wait_lines(9, 1, r_lat.at[5])

    convolve(jnp.where(core == 0, 0, 5), 3)

    for a in range(3):
        wait_bytes(kbuf.at[pl.ds(0, 15 * BLOCK), :], s_qkv.at[a])

    @pl.when(jnp.logical_not(last))
    def _():
        wait_bytes(kbuf.at[pl.ds(0, 2 * WIN), :], s_halo.at[0])

    @pl.when(jnp.logical_not(first))
    def _():
        wait_bytes(kbuf.at[pl.ds(0, 2 * WIN), :], s_halo.at[1])

    wait_bytes(wq.at[pl.ds(0, 3 * PIECE), pl.ds(0, HALF)], s_w.at[0])
    wait_bytes(wq.at[pl.ds(0, 9 * PIECE), pl.ds(0, HALF)], s_w.at[1])
    wait_bytes(wq.at[pl.ds(0, 3 * SHARD), pl.ds(0, HALF)], s_w.at[2])
    wait_bytes(rbuf.at[pl.ds(0, 3)], s_res.at[0])
    wait_bytes(mbuf.at[pl.ds(0, 3)], s_res.at[1])
    wait_bytes(att.at[pl.ds(0, 3)], s_g.at[0])
    wait_bytes(gbuf.at[:, :, pl.ds(0, 3 * 512)], s_y.at[0])
    wait_bytes(msg.at[pl.ds(0, 3)], s_msg.at[0])
    for _, finish in hands:
        finish()


def on_device(
    queries,
    head_keys,
    head_values,
    region_request,
    request_adapter,
    residual,
    output_gate,
    output_weight,
    adapter_down_factors,
    adapter_up_factors,
    closing_scale,
    closing_shift,
    patch_projection_weight,
    patch_projection_bias,
    convolution_kernel,
    convolution_bias,
):
    far = pl.BlockSpec(memory_space=pl.ANY)
    near = pl.BlockSpec(memory_space=pltpu.VMEM)
    scalars = pl.BlockSpec(memory_space=pltpu.SMEM)
    dma = pltpu.SemaphoreType.DMA
    return pl.pallas_call(
        kernel,
        out_shape=jax.ShapeDtypeStruct((16, 32, 512), BF16),
        in_specs=[
            far, far, far, near, scalars, far, near, far,
            near, far, near, near, near, near, near, near,
        ],
        out_specs=near,
        scratch_shapes=[
            pltpu.VMEM((BAND, HD), BF16),
            pltpu.VMEM((BAND + 2 * WIN, HD), BF16),
            pltpu.VMEM((BAND + 2 * WIN, HD), BF16),
            pltpu.VMEM((4, 4, BLOCK, HD), BF16),
            pltpu.VMEM((QUARTER, PAD_DEEP), BF16),
            pltpu.VMEM((128, QUARTER), BF16),
            pltpu.VMEM((4, BLOCK, QUARTER), BF16),
            pltpu.VMEM((4, BLOCK, RANKS), BF16),
            pltpu.VMEM((4, BLOCK, DEEP), BF16),
            pltpu.VMEM((BLOCK, QUARTER), F32),
            pltpu.VMEM((4, 80, 128), F32),
            pltpu.VMEM((4, 80, 128), F32),
            pltpu.VMEM((BLOCK, 128), BF16),
            pltpu.VMEM((10, 48, 128), BF16),
            pltpu.VMEM((10, 48, 128), F32),
            pltpu.VMEM((4, 512, 512), BF16),
            pltpu.VMEM((4, 16, 32, 128), F32),
            pltpu.VMEM((8, 128), F32),
            dma((3, 4)),
            dma((3,)),
            dma((2,)),
            dma((2,)),
            dma((2,)),
            dma((3,)),
            dma((3,)),
            dma((2,)),
            dma((2,)),
            dma((4, 4)),
            dma((1,)),
            dma((4,)),
            dma((1,)),
            dma((1,)),
            dma((1,)),
            dma((6,)),
            dma((27,)),
        ],
        compiler_params=pltpu.CompilerParams(
            collective_id=0, has_side_effects=True, vmem_limit_bytes=60 * 1024 * 1024
        ),
    )(
        queries,
        head_keys,
        head_values,
        region_request.reshape(1, -1),
        request_adapter,
        residual,
        output_gate.reshape(1, -1),
        output_weight.T,
        adapter_down_factors,
        adapter_up_factors.T,
        closing_scale.reshape(1, -1),
        closing_shift.reshape(1, -1),
        patch_projection_weight.T,
        patch_projection_bias.reshape(1, -1),
        convolution_kernel,
        convolution_bias.reshape(1, -1),
    )


def solution(mesh):
    return jax.shard_map(
        on_device,
        mesh=mesh,
        in_specs=(
            P(("seq", "tile"), None),
            P(("seq", "tile"), None),
            P(("seq", "tile"), None),
            P(("seq", "tile")),
            P(),
            P(("seq", "tile"), None),
            P(),
            P(None, "tile"),
            P(),
            P(None, "tile"),
            P(),
            P(),
            P(),
            P(),
            P(),
            P(),
        ),
        out_specs=P("seq", "tile", None),
        check_vma=False,
    )
```
